256 devices in a mesh: lat: 32 (over x_hi, z, core), lon: 8 (over x_lo, y).
Axes of the slice: x: 4 (x_hi: 2, x_lo: 2; x = x_hi * 2 + x_lo), y: 4, z: 8, core: 2. Of those that a mesh axis runs over, the one named last changes fastest.
Arguments:
- input_field: bfloat16 [1, 384, 192, 1024], P(None, 'lat', None, 'lon'), may hold values from -6 to 6
- basis_values: float32 [384, 5, 5, 9], replicated, may hold values from -1.75 to 1.75
- support_reach: int32 [384, 5], replicated, may hold values from 0 to 2
- mix_weight: bfloat16 [4, 9, 48, 48], replicated, may hold values from -0.3125 to 0.3125
- filter_weight: float32 [384, 192], replicated, may hold values from -6 to 6
- cotangent: bfloat16 [1, 384, 192, 1024], P(None, 'lat', None, 'lon'), may hold values from -6 to 6
Outputs:
- block_out: bfloat16 [1, 384, 192, 1024], P(None, 'lat', None, 'lon')
- grad_field: bfloat16 [1, 384, 192, 1024], P(None, 'lat', None, 'lon')
The draws below stay inside these ranges and needn't reach their ends.
Inputs may be any that keep to these rules, and one draw needn't show every extreme that they name: support_reach[i, a] is how many longitude cells on each side the filter reaches at latitude offset a - 2 from row i.
All inputs are finite; a program needn't handle non-finite values.
Results may differ from the reference program's by a relative error of at most 0.011.
Values may be sent and summed in bfloat16 or wider, within the bound.
No kernel may reach another device: no remote copies, remote signals or barrier semaphores. Data moves between devices by JAX's collectives and lax.ppermute only.
A program may use at most 192 MiB of HBM per device.

```python
import math
import jax
import jax.numpy as jnp
from jax import lax

NLAT = 384
NLON = 1024
LMAX = 384
C = 192
GROUPS = 4
KB = 9
HALO = 2
SAMPLES = 1
CG = 48
SPAN = 5


def touch_ends(entries, key, least, high):
    place = [jax.random.randint(jax.random.fold_in(key, axis), (), 0, length) for axis, length in enumerate(entries.shape)]
    longest = entries.shape.index(max(entries.shape))
    next_to = place[:longest] + [(place[longest] + 1) % entries.shape[longest]] + place[longest + 1:]
    return entries.at[tuple(place)].set(least).at[tuple(next_to)].set(high)


def block_scale(own_key, extent, shards, least, top_value):
    gain = 1.0
    for position, blocks in shards:
        heights = jax.random.uniform(jax.random.fold_in(jax.random.fold_in(own_key, 6), position), (blocks,), jnp.float32, least / len(shards), top_value / len(shards))
        gain = gain * jnp.repeat(jnp.exp(heights), extent[position] // blocks).reshape((-1,) + (1,) * (len(extent) - 1 - position))
    return gain


def centred(key, shape, deviation, bound, pieces=(), kind=jnp.bfloat16):
    array = deviation * jax.random.normal(key, shape, jnp.float32)
    if pieces:
        array = array * block_scale(key, shape, pieces, -0.22, 0.18)
    return jnp.clip(array, -bound, bound).astype(kind)


def setup_inputs(seed: int = 0) -> dict:
    splits = jax.random.split(jax.random.key(seed), 7)
    input_field = centred(splits[0], (SAMPLES, NLAT, C, NLON), 1.0, 6.0, ((1, 32), (3, 8)))
    basis_values = centred(splits[1], (NLAT, SPAN, SPAN, KB), 0.3, 1.75, (), jnp.float32)
    support_reach = touch_ends(jax.random.randint(splits[2], (NLAT, SPAN), 0, HALO + 1), jax.random.fold_in(splits[2], 1), 0, HALO).astype(jnp.int32)
    mix_weight = centred(splits[3], (GROUPS, KB, CG, CG), (KB * CG) ** -0.5, 0.3125)
    filter_weight = centred(splits[4], (LMAX, C), 1.0, 6.0, (), jnp.float32)
    cotangent = centred(splits[5], (SAMPLES, NLAT, C, NLON), 1.0, 6.0, ((1, 32), (3, 8)))
    return {"input_field": input_field, "basis_values": basis_values, "support_reach": support_reach, "mix_weight": mix_weight, "filter_weight": filter_weight, "cotangent": cotangent}


huge_value = 2.0 ** 60
tiny_value = 2.0 ** (-60)
log_step = 41.58883083359672

def colatitude(nlat_total):
    return math.pi * (jnp.arange(nlat_total, dtype=jnp.float32) + 0.5) / nlat_total

def quadrature(nlat_total, nlon_total):
    return 2.0 * math.pi * math.pi / nlat_total * jnp.sin(colatitude(nlat_total)) / nlon_total

def order_scale(orders):
    return jnp.where(orders == 0, 1.0, 2.0).astype(jnp.float32)

def lon_table(degree_count, nlon_total):
    product = jnp.arange(nlon_total, dtype=jnp.int32)[:, None] * jnp.arange(degree_count, dtype=jnp.int32)[None, :]
    phase_angle = 2.0 * math.pi / nlon_total * (product % nlon_total).astype(jnp.float32)
    cosine = jnp.cos(phase_angle).astype(jnp.bfloat16)
    sine_part = jnp.sin(phase_angle).astype(jnp.bfloat16)
    return jnp.stack([cosine, -sine_part], axis=1)

def legendre(orders, degree_count, nlat_total):
    colat_angle = colatitude(nlat_total)
    cosine = jnp.cos(colat_angle)[None, :]
    log_sine = jnp.log(jnp.sin(colat_angle))[None, :]
    counter = jnp.arange(1, degree_count, dtype=jnp.float32)
    running = jnp.cumsum(jnp.log((2.0 * counter - 1.0) / (2.0 * counter)))
    cumulative = jnp.concatenate([jnp.zeros((1,), jnp.float32), running])
    select = (orders[:, None] == jnp.arange(degree_count, dtype=jnp.int32)[None, :]).astype(jnp.float32)
    norm_log = lax.optimization_barrier(jnp.sum(select * cumulative[None, :], axis=1))
    order_real = orders.astype(jnp.float32)[:, None]
    base_log = 0.5 * jnp.log((2.0 * order_real + 1.0) / (4.0 * math.pi)) + 0.5 * norm_log[:, None] + order_real * log_sine
    empty_state = jnp.zeros((orders.shape[0], nlat_total), jnp.float32)

    def advance(carry, degree):
        latest, earlier, exponent = carry
        degree_real = degree.astype(jnp.float32)
        forward_gain = jnp.sqrt(jnp.maximum(4.0 * degree_real * degree_real - 1.0, 1.0) / jnp.maximum(degree_real * degree_real - order_real * order_real, 1.0))
        back_gain = jnp.sqrt(jnp.maximum((degree_real - 1.0) ** 2 - order_real * order_real, 0.0) / jnp.maximum(4.0 * (degree_real - 1.0) ** 2 - 1.0, 1.0))
        fresh = forward_gain * (cosine * latest - back_gain * earlier)
        start_here = degree == orders[:, None]
        fresh = jnp.where(start_here, 1.0, fresh)
        fresh = jnp.where(degree >= orders[:, None], fresh, 0.0)
        grown = jnp.abs(fresh) > huge_value
        fresh = jnp.where(grown, fresh * tiny_value, fresh)
        earlier_next = jnp.where(grown, latest * tiny_value, latest)
        exponent = exponent + grown.astype(jnp.float32)
        result_value = fresh * jnp.exp(base_log + exponent * log_step)
        return ((fresh, earlier_next, exponent), result_value.astype(jnp.bfloat16))
    degrees = jnp.arange(degree_count, dtype=jnp.int32)
    unused_carry, table = lax.scan(advance, (empty_state, empty_state, empty_state), degrees, unroll=16)
    return table

def stencil_weights(basis_values, support_reach):
    rim_width = basis_values.shape[1] // 2
    offsets = jnp.abs(jnp.arange(basis_values.shape[2], dtype=jnp.int32) - rim_width)
    inside = (offsets[None, None, :] <= support_reach[:, :, None]).astype(jnp.float32)
    return basis_values * inside[:, :, :, None]

def pad_grid(grid_in, rim_width):
    padded = jnp.pad(grid_in, ((0, 0), (rim_width, rim_width), (0, 0), (0, 0)))
    return jnp.concatenate([padded[..., -rim_width:], padded, padded[..., :rim_width]], axis=3)

def basis_response(padded, weights_rows, basis_index, row_count, col_count):
    span_count = weights_rows.shape[1]
    total = jnp.zeros((padded.shape[0], row_count, padded.shape[2], col_count), jnp.float32)
    for lat_shift in range(span_count):
        for lon_shift in range(span_count):
            factor = weights_rows[:, lat_shift, lon_shift, basis_index][None, :, None, None]
            window = padded[:, lat_shift:lat_shift + row_count, :, lon_shift:lon_shift + col_count]
            total = total + factor * window.astype(jnp.float32)
    return total

def adjoint_response(padded, weights_padded, basis_index, row_count, col_count):
    span_count = weights_padded.shape[1]
    last_shift = span_count - 1
    total = jnp.zeros((padded.shape[0], row_count, padded.shape[2], col_count), jnp.float32)
    for lat_shift in range(span_count):
        for lon_shift in range(span_count):
            first_row = last_shift - lat_shift
            first_col = last_shift - lon_shift
            factor = weights_padded[first_row:first_row + row_count, lat_shift, lon_shift, basis_index][None, :, None, None]
            window = padded[:, first_row:first_row + row_count, :, first_col:first_col + col_count]
            total = total + factor * window.astype(jnp.float32)
    return total

def spectral(grid_in, lon_tab, table, gains, pre_rows, pre_orders, post_rows, post_orders):
    exact_mode = lax.Precision.HIGHEST
    lon_spec = jnp.einsum('sicj,jrm->sicrm', grid_in.astype(jnp.float32), lon_tab.astype(jnp.float32), precision=exact_mode)
    lon_spec = (lon_spec * pre_rows[None, :, None, None, None] * pre_orders[None, None, None, None, :]).astype(jnp.bfloat16)
    coeffs = jnp.einsum('stcrm,lmt->scrml', lon_spec.astype(jnp.float32), table.astype(jnp.float32), precision=exact_mode)
    filtered = (coeffs * jnp.transpose(gains)[None, :, None, None, :]).astype(jnp.bfloat16)
    synthesis = jnp.einsum('scrml,lmt->stcrm', filtered.astype(jnp.float32), table.astype(jnp.float32), precision=exact_mode)
    synthesis = (synthesis * post_rows[None, :, None, None, None] * post_orders[None, None, None, None, :]).astype(jnp.bfloat16)
    circle_out = jnp.einsum('sicrm,jrm->sicj', synthesis.astype(jnp.float32), lon_tab.astype(jnp.float32), precision=exact_mode)
    return circle_out.astype(jnp.bfloat16)

def reference(input_field, basis_values, support_reach, mix_weight, filter_weight, cotangent):
    exact_mode = lax.Precision.HIGHEST
    samples, nlat_total, channels, nlon_total = input_field.shape
    rim_width = basis_values.shape[1] // 2
    groups = mix_weight.shape[0]
    basis_count = mix_weight.shape[1]
    group_width = mix_weight.shape[2]
    degree_count = filter_weight.shape[0]
    weights_all = stencil_weights(basis_values, support_reach)
    padded_field = pad_grid(input_field, rim_width)
    conv_out = jnp.zeros((samples, nlat_total, groups, group_width, nlon_total), jnp.float32)
    for basis_index in range(basis_count):
        response = basis_response(padded_field, weights_all, basis_index, nlat_total, nlon_total).astype(jnp.bfloat16)
        response = response.reshape(samples, nlat_total, groups, group_width, nlon_total)
        conv_out = conv_out + jnp.einsum('sigcj,gco->sigoj', response.astype(jnp.float32), mix_weight[:, basis_index].astype(jnp.float32), precision=exact_mode)
    conv_out = conv_out.reshape(samples, nlat_total, channels, nlon_total)
    activated = jax.nn.gelu(conv_out).astype(jnp.bfloat16)
    lon_tab = lon_table(degree_count, nlon_total)
    table = legendre(jnp.arange(degree_count, dtype=jnp.int32), degree_count, nlat_total)
    quad_all = quadrature(nlat_total, nlon_total)
    order_all = order_scale(jnp.arange(degree_count, dtype=jnp.int32))
    ones_rows = jnp.ones((nlat_total,), jnp.float32)
    ones_orders = jnp.ones((degree_count,), jnp.float32)
    branch = spectral(activated, lon_tab, table, filter_weight, quad_all, ones_orders, ones_rows, order_all)
    block_out = (input_field.astype(jnp.float32) + branch.astype(jnp.float32)).astype(jnp.bfloat16)
    cot_act = spectral(cotangent, lon_tab, table, filter_weight, ones_rows, order_all, quad_all, ones_orders)
    slope = jax.vjp(jax.nn.gelu, conv_out)[1](cot_act.astype(jnp.float32))[0]
    cot_conv = slope.astype(jnp.bfloat16)
    grouped = cot_conv.reshape(samples, nlat_total, groups, group_width, nlon_total).astype(jnp.float32)
    weights_padded = jnp.pad(weights_all, ((rim_width, rim_width), (0, 0), (0, 0), (0, 0)))
    cot_field = jnp.zeros((samples, nlat_total, channels, nlon_total), jnp.float32)
    for basis_index in range(basis_count):
        mixed = jnp.einsum('sigoj,gco->sigcj', grouped, mix_weight[:, basis_index].astype(jnp.float32), precision=exact_mode)
        mixed = mixed.reshape(samples, nlat_total, channels, nlon_total).astype(jnp.bfloat16)
        cot_field = cot_field + adjoint_response(pad_grid(mixed, rim_width), weights_padded, basis_index, nlat_total, nlon_total)
    grad_field = (cotangent.astype(jnp.float32) + cot_field).astype(jnp.bfloat16)
    return (block_out, grad_field)
```

```python
import functools
import math

import jax
import jax.numpy as jnp
import numpy as np
from jax import lax
from jax.experimental import pallas as pl
from jax.experimental.pallas import tpu as pltpu
from jax.sharding import PartitionSpec as P

huge_value = 2.0**60
tiny_value = 2.0 ** (-60)
log_step = 41.58883083359672

f32 = jnp.float32
bf16 = jnp.bfloat16

NT = (((1,), (1,)), ((), ()))
NN = (((1,), (0,)), ((), ()))
TN = (((0,), (0,)), ((), ()))


def dot(a, b, dims=NN):
    return lax.dot_general(a, b, dims, preferred_element_type=f32)


def params(mib=20):
    return pltpu.CompilerParams(vmem_limit_bytes=mib * 1024 * 1024)


def vmem(count):
    return [pl.BlockSpec(memory_space=pltpu.VMEM)] * count


def cost(flops, nbytes):
    return pl.CostEstimate(flops=int(flops), bytes_accessed=int(nbytes), transcendentals=0)


def legendre_kernel(
    m_count, idx_ref, rise_ref, fall_ref, norm_ref, cos_ref, logsin_ref, table_ref, flip_ref, keep
):
    m_pad, lat = norm_ref.shape[0], cos_ref.shape[1]
    degrees = table_ref.shape[1]
    wide = lat // 128
    first = idx_ref[0] * m_count
    order = first + lax.broadcasted_iota(jnp.int32, (m_pad, 128), 0)
    order_real = order.astype(f32)
    square = order_real * order_real
    cosine = [
        jnp.broadcast_to(cos_ref[:, p * 128 : (p + 1) * 128], (m_pad, 128)) for p in range(wide)
    ]
    base = [
        norm_ref[...] + order_real * logsin_ref[:, p * 128 : (p + 1) * 128] for p in range(wide)
    ]

    def block(number, carry):
        latest, earlier, exponent, gain_b = carry
        latest, earlier, exponent = list(latest), list(earlier), list(exponent)
        for step in range(16):
            degree = number * 16 + step
            if step % 4 == 0:
                scale = []
                for p in range(wide):
                    grown = jnp.abs(latest[p]) > huge_value
                    latest[p] = jnp.where(grown, latest[p] * tiny_value, latest[p])
                    earlier[p] = jnp.where(grown, earlier[p] * tiny_value, earlier[p])
                    exponent[p] = jnp.where(grown, exponent[p] + 1.0, exponent[p])
                    scale.append(jnp.exp(base[p] + exponent[p] * log_step))
            d = degree.astype(f32)
            width = d * d - square
            inverse = lax.rsqrt(jnp.maximum(width, 1.0))
            gain_a = rise_ref[degree] * inverse
            both = gain_a * gain_b
            start_here = order == degree
            for p in range(wide):
                fresh = (gain_a * cosine[p]) * latest[p] - both * earlier[p]
                fresh = jnp.where(start_here, 1.0, fresh)
                earlier[p] = latest[p]
                latest[p] = fresh
                keep[p, step * m_pad : (step + 1) * m_pad, :] = fresh * scale[p]
            gain_b = fall_ref[degree] * (jnp.maximum(width, 0.0) * inverse)
        for m in range(m_count):
            rows = jnp.concatenate(
                [keep[part, pl.ds(m, 16, stride=m_pad), :] for part in range(wide)], axis=1
            )
            table_ref[m, pl.ds(pl.multiple_of(number * 16, 16), 16), :] = rows.astype(bf16)
        return tuple(latest), tuple(earlier), tuple(exponent), gain_b

    zero = jnp.zeros((m_pad, 128), f32)
    zeros = (zero,) * wide
    lax.fori_loop(0, degrees // 16, block, (zeros, zeros, zeros, zero))

    def turn(m, carry):
        flip_ref[m] = jnp.transpose(table_ref[m])
        return carry

    lax.fori_loop(0, m_count, turn, 0)


def legendre_tables(lat_index, degrees, lat_count, row_count, m_count):
    nlat = lat_count * row_count
    m_pad = 16
    place = np.arange(nlat)
    t = (place % lat_count) * row_count + place // lat_count
    theta = math.pi * (t + 0.5) / nlat
    counter = np.arange(1, degrees, dtype=np.float64)
    running = np.concatenate([[0.0], np.cumsum(np.log((2 * counter - 1) / (2 * counter)))])
    m = np.arange(degrees)
    norm = 0.5 * np.log((2 * m + 1) / (4 * math.pi)) + 0.5 * running
    norms = np.zeros((lat_count, m_pad, 1), np.float32)
    norms[:, :m_count, 0] = norm.reshape(lat_count, m_count)
    norm_mine = lax.dynamic_index_in_dim(jnp.asarray(norms), lat_index, 0, keepdims=False)
    rise = np.sqrt(np.maximum(4.0 * m * m - 1.0, 1.0)).astype(np.float32)
    fall = (1.0 / np.sqrt(np.maximum(4.0 * m * m - 1.0, 1.0))).astype(np.float32)
    shape = jax.ShapeDtypeStruct((m_count, degrees, nlat), bf16)
    flip = jax.ShapeDtypeStruct((m_count, nlat, degrees), bf16)
    return pl.pallas_call(
        functools.partial(legendre_kernel, m_count),
        out_shape=(shape, flip),
        in_specs=[pl.BlockSpec(memory_space=pltpu.SMEM)] * 3 + vmem(3),
        out_specs=tuple(vmem(2)),
        scratch_shapes=[pltpu.VMEM((nlat // 128, 16 * m_pad, 128), f32)],
        compiler_params=params(),
        cost_estimate=cost(2e9, 7e6),
        name="legendre_tables",
    )(
        lat_index[None],
        jnp.asarray(rise),
        jnp.asarray(fall),
        norm_mine,
        jnp.asarray(np.cos(theta)[None].astype(np.float32)),
        jnp.asarray(np.log(np.sin(theta))[None].astype(np.float32)),
    )


def lon_kernel(near_cos_ref, near_sin_ref, far_ref, tab_ref):
    blocks = tab_ref.shape[1] // 128
    for b in range(blocks):
        tab_ref[:, b * 128 : (b + 1) * 128] = (
            near_cos_ref[...] * far_ref[:, b : b + 1]
            - near_sin_ref[...] * far_ref[:, blocks + b : blocks + b + 1]
        ).astype(bf16)


def lon_table(degrees, nlon, owners):
    per = degrees // owners
    row = np.arange(2 * degrees)
    m_np = row // (2 * per) * per + row % per
    m = jnp.asarray(m_np.astype(np.int32))
    shift = jnp.asarray(((row // per % 2) * (nlon // 4)).astype(np.int32))
    low = jnp.arange(128, dtype=jnp.int32)
    angle = (m[:, None] * low[None, :] + shift[:, None]) % nlon
    phase = 2.0 * math.pi / nlon * angle.astype(f32)
    far = 2.0 * math.pi * ((m_np[:, None] * np.arange(nlon // 128)[None] * 128) % nlon) / nlon
    far = np.concatenate([np.cos(far), np.sin(far)], axis=1).astype(np.float32)
    return pl.pallas_call(
        lon_kernel,
        out_shape=jax.ShapeDtypeStruct((2 * degrees, nlon), bf16),
        in_specs=vmem(3),
        out_specs=vmem(1)[0],
        compiler_params=params(),
        cost_estimate=cost(1e8, 3e6),
        name="lon_table",
    )(jnp.cos(phase), jnp.sin(phase), jnp.asarray(far))


def pack_rows(z, k_count):
    third = k_count // 3
    rest = [z[j * third : (j + 1) * third, 256:288] for j in range(3)]
    rest.append(jnp.zeros((third, 32), f32))
    return jnp.concatenate([z[:, 0:128], z[:, 128:256], jnp.concatenate(rest, axis=1)], axis=0)


def analysis_kernel(k_count, cotangent_pass, *refs):
    circ_ref, tab_ref, quad_ref = refs[:3]
    out_ref, keep = refs[-2:]
    sectors = circ_ref.shape[0]
    lines = keep.shape[1]
    owners = out_ref.shape[0]
    height = 2 * k_count + k_count // 3
    if len(circ_ref.shape) == 3:
        parts = [circ_ref[s, 0:lines, :] for s in range(sectors)]
    else:
        parts = [circ_ref[s].astype(f32).reshape(lines, -1).astype(bf16) for s in range(sectors)]
    circ = jnp.concatenate(parts, axis=1)
    z = dot(tab_ref[...], circ, NT)
    if cotangent_pass:
        row = lax.broadcasted_iota(jnp.int32, z.shape, 0)
        z = z * jnp.where((row == 0) | (row == k_count // 2), 1.0, 2.0)
    else:
        z = z * quad_ref[...]
    keep[...] = z
    for e in range(owners):
        piece = keep[e * k_count : (e + 1) * k_count, :]
        out_ref[e, 0:height, :] = pack_rows(piece, k_count).astype(bf16)
        if len(refs) > 5:
            out_ref[e, height:, :] = refs[3][e]


def analysis(circ, lines, tab, quad_lanes, owners, cotangent_pass, beside=()):
    k_count = tab.shape[0] // owners
    height = (2 * k_count + k_count // 3) * (1 + len(beside))
    return pl.pallas_call(
        functools.partial(analysis_kernel, k_count, cotangent_pass),
        out_shape=jax.ShapeDtypeStruct((owners, height, 128), bf16),
        in_specs=vmem(3 + len(beside)),
        out_specs=vmem(1)[0],
        scratch_shapes=[pltpu.VMEM((tab.shape[0], lines), f32)],
        compiler_params=params(),
        cost_estimate=cost(2 * tab.shape[0] * tab.shape[1] * lines, 3e6),
        name="analysis",
    )(circ, tab, quad_lanes, *beside)


def filter_kernel(
    m_count, chans, cotangent_pass, idx_ref, recv_ref, table_ref, flip_ref, gain_ref, post_ref,
    out_ref, took, give
):
    places, height, _ = out_ref.shape
    k_count = 2 * m_count
    third = k_count // 3
    nlat = table_ref.shape[1]
    rows = nlat // places
    lane = lax.broadcasted_iota(jnp.int32, (places, 128), 1)

    def load(d, carry):
        at = pl.ds(pl.multiple_of(d * height, 8), height)
        took[at, :] = recv_ref[d, 0:height, :].astype(f32)
        return carry

    lax.fori_loop(0, places, load, 0, unroll=4)
    give[2 * k_count * places :, :] = jnp.zeros((third * places, 128), f32)

    def one(mm, carry):
        blocks = []
        for r in range(2):
            k = r * m_count + mm
            b0 = took[pl.ds(k, places, stride=height), :]
            b1 = took[pl.ds(k_count + k, places, stride=height), :]
            b2 = took[pl.ds(2 * k_count + k % third, places, stride=height), :]
            b2 = pltpu.roll(b2, (128 - 32 * (k // third)) % 128, 1)
            blocks.append((b0, b1, b2))
        columns = []
        for i in range(rows):
            start = i * chans
            first, last = start // 128, (start + chans - 1) // 128
            total = None
            for q, b in enumerate(blocks):
                if first == last:
                    source = b[first]
                else:
                    source = jnp.where(lane < 64, b[last], b[first])
                shift = (q * chans - start) % 128
                source = pltpu.roll(source, shift, 1) if shift else source
                total = source if total is None else jnp.where(lane < chans, total, source)
            columns.append(total)
        x = jnp.concatenate(columns, axis=0).astype(bf16)
        coeffs = dot(table_ref[mm], x)
        filtered = (coeffs * gain_ref[...]).astype(bf16)
        y = dot(flip_ref[mm], filtered)
        if cotangent_pass:
            y = y * post_ref[...]
        else:
            y = y * jnp.where(idx_ref[0] * m_count + mm == 0, 1.0, 2.0).astype(f32)
        for r in range(2):
            k = r * m_count + mm
            outs = [jnp.zeros((places, 128), f32) for _ in range(3)]
            for i in range(rows):
                start = i * chans
                first, last = start // 128, (start + chans - 1) // 128
                shift = (start - r * chans) % 128
                piece = y[i * places : (i + 1) * places, :]
                piece = pltpu.roll(piece, shift, 1) if shift else piece
                for part in range(first, last + 1):
                    lo, hi = start - part * 128, start + chans - part * 128
                    outs[part] = jnp.where((lane >= lo) & (lane < hi), piece, outs[part])
            give[pl.ds(k * places, places), :] = outs[0]
            give[pl.ds((k_count + k) * places, places), :] = outs[1]
            at = pl.ds((2 * k_count + k % third) * places, places)
            give[at, :] = give[at, :] + pltpu.roll(outs[2], 32 * (k // third), 1)
        return carry

    lax.fori_loop(0, m_count, one, 0, unroll=2)

    def store(d, carry):
        out_ref[d] = give[pl.ds(d, height, stride=places), :].astype(bf16)
        return carry

    lax.fori_loop(0, places, store, 0, unroll=4)


def filter_step(lat_index, recv, table, flip, gains, post, chans, cotangent_pass):
    places = recv.shape[0]
    m_count, degrees, nlat = table.shape
    height = 4 * m_count + 2 * m_count // 3
    return pl.pallas_call(
        functools.partial(filter_kernel, m_count, chans, cotangent_pass),
        out_shape=jax.ShapeDtypeStruct((places, height, 128), bf16),
        in_specs=[pl.BlockSpec(memory_space=pltpu.SMEM)] + vmem(5),
        out_specs=vmem(1)[0],
        scratch_shapes=[
            pltpu.VMEM((places * height, 128), f32),
            pltpu.VMEM((places * height, 128), f32),
        ],
        compiler_params=params(),
        cost_estimate=cost(4 * m_count * degrees * nlat * 128, 9e6),
        name="filter_step",
    )(lat_index[None], recv, table, flip, gains, post)


def synthesis_kernel(which, recv_ref, tab_ref, out_ref):
    owners = recv_ref.shape[0]
    k_count = tab_ref.shape[0] // owners
    height = 2 * k_count + k_count // 3
    sectors, rows, chans, cols = out_ref.shape
    left, middle, right = [], [], []
    for e in range(owners):
        v = recv_ref[e, which * height : (which + 1) * height, :].astype(f32)
        left.append(v[0:k_count])
        middle.append(v[k_count : 2 * k_count])
        rest = v[2 * k_count :]
        for j in range(3):
            right.append(pltpu.roll(rest, (128 - 32 * j) % 128, 1) if j else rest)
    flat = [jnp.transpose(jnp.concatenate(part, axis=0)) for part in (left, middle, right)]
    s = jnp.concatenate([flat[0], flat[1], flat[2][0:32]], axis=0).astype(bf16)
    circ = dot(s, tab_ref[...])
    for sector in range(sectors):
        piece = circ[:, sector * cols : (sector + 1) * cols]
        out_ref[sector] = piece.reshape(rows, chans, cols).astype(bf16)


def synthesis(recv, tab, which, shape):
    return pl.pallas_call(
        functools.partial(synthesis_kernel, which),
        out_shape=jax.ShapeDtypeStruct(shape, bf16),
        in_specs=vmem(2),
        out_specs=vmem(1)[0],
        compiler_params=params(),
        cost_estimate=cost(2 * tab.shape[0] * tab.shape[1] * shape[1] * shape[2], 5e6),
        name="synthesis",
    )(recv, tab)


def chunk_blocks(count, edge):
    inner = list(range(edge, count - edge))
    return (
        [list(range(edge))]
        + [inner[k : k + 4] for k in range(0, len(inner), 4)]
        + [list(range(count - edge, count))]
    )


def edge_blocks(flat, edge):
    row = lax.broadcasted_iota(jnp.int32, (16, 128), 0)
    lane = lax.broadcasted_iota(jnp.int32, (16, 128), 1)
    first = []
    last = []
    for chunks in chunk_blocks(flat.shape[0] // 128, edge):
        total = jnp.zeros((16, 128), f32)
        for v, chunk in enumerate(chunks):
            head = (row == 2 * v + lane) & (lane < 2)
            tail = (row - 8 - 2 * v == lane - 126) & (lane >= 126)
            select = jnp.where(head | tail, 1.0, 0.0).astype(bf16)
            total = total + dot(select, flat[chunk * 128 : (chunk + 1) * 128], NT)
        first.append(total[0:8])
        last.append(total[8:16])
    return jnp.concatenate(first, axis=0), jnp.concatenate(last, axis=0)


def start_kernel(edge, idx_ref, cot_ref, field_ref, out_ref):
    sectors, height, cols = out_ref.shape
    rows, channels, _ = cot_ref.shape
    chans = channels // sectors
    body = rows * chans
    field = field_ref[...].reshape(rows * channels, cols)
    first, last = edge_blocks(field, edge)
    for b in range(sectors):
        parts = [cot_ref[i, b * chans : (b + 1) * chans, :].astype(f32) for i in range(rows)]
        right = lax.rem(idx_ref[0] + 1, sectors) == b
        parts.append(jnp.where(right, last, first))
        room = height - body - first.shape[0]
        parts.append(jnp.zeros((room, cols), f32))
        out_ref[b] = jnp.concatenate(parts, axis=0).astype(bf16)


def start_step(lon_index, cot, field, sectors, edge):
    rows, channels, cols = cot.shape
    body = rows * channels // sectors
    blocks = len(chunk_blocks(rows * channels // 128, edge))
    height = -(-(body + 8 * blocks) // 16) * 16
    return pl.pallas_call(
        functools.partial(start_kernel, edge),
        out_shape=jax.ShapeDtypeStruct((sectors, height, cols), bf16),
        in_specs=[pl.BlockSpec(memory_space=pltpu.SMEM)] + vmem(2),
        out_specs=vmem(1)[0],
        compiler_params=params(),
        cost_estimate=cost(1e8, 2e6),
        name="start",
    )(lon_index[None], cot, field)


def conv_body(
    idx_ref, x_ref, low_ref, high_ref, left_ref, right_ref, stencil_ref, mix_ref,
    xs, hs, resp, band, blend, emit
):
    rows, channels, cols = x_ref.shape
    groups, taps, width = mix_ref.shape[0], mix_ref.shape[1] // mix_ref.shape[2], mix_ref.shape[2]
    ext = hs.shape[0] // channels
    rim = (ext - rows) // 2
    span = 2 * rim + 1
    edge = rim * channels // 128
    k_pad = 16
    xs[0 : rim * channels, :] = low_ref[0 : rim * channels].astype(f32)
    xs[rim * channels : (rim + rows) * channels, :] = (
        x_ref[...].astype(f32).reshape(rows * channels, cols)
    )
    xs[(rim + rows) * channels :, :] = high_ref[0 : rim * channels].astype(f32)

    row = lax.broadcasted_iota(jnp.int32, (16, cols), 0)
    lane = lax.broadcasted_iota(jnp.int32, (16, cols), 1)

    def spread(left, right, chunks, base):
        turned = jnp.transpose(jnp.concatenate([left.astype(f32), right.astype(f32)], axis=0))
        turned = turned.astype(bf16)
        for v, chunk in enumerate(chunks):
            ahead = (row - 2 * v == lane - (cols - 2)) & (lane >= cols - 2)
            behind = (row - 8 - 2 * v == lane) & (lane < 2)
            put = jnp.where(ahead | behind, 1.0, 0.0).astype(bf16)
            at = (base + chunk) * 128
            hs[at : at + 128, :] = dot(turned, put)

    lists = chunk_blocks(rows * channels // 128, edge)
    tail = rim * channels
    spread(low_ref[tail : tail + 8], low_ref[tail + 8 : tail + 16], range(edge), 0)
    spread(high_ref[tail : tail + 8], high_ref[tail + 8 : tail + 16], range(edge),
           edge + rows * channels // 128)
    for u, chunks in enumerate(lists):
        at = slice(8 * u, 8 * u + 8)
        spread(left_ref[at], right_ref[at], chunks, edge)

    tap = lax.broadcasted_iota(jnp.int32, (stencil_ref.shape[1], 128), 0)
    slot = lax.broadcasted_iota(jnp.int32, (stencil_ref.shape[1], 128), 1)
    source = idx_ref[0] * rows - rim + slot % ext
    inside = (source >= 0) & (source < idx_ref[1]) & (slot < span * ext)
    for i in range(rows):
        hit = inside & (tap // span == slot // ext) & (slot % ext == i + tap % span)
        place = jnp.where(hit, 1.0, 0.0).astype(bf16)
        band[i * k_pad : (i + 1) * k_pad, :] = dot(
            stencil_ref[i * k_pad : (i + 1) * k_pad, :], place
        ).astype(bf16)

    depth = width * k_pad
    pair_row = lax.broadcasted_iota(jnp.int32, (taps * width, depth), 0)
    pair_lane = lax.broadcasted_iota(jnp.int32, (taps * width, depth), 1)
    place = jnp.where(
        pair_lane == (pair_row % width) * k_pad + pair_row // width, 1.0, 0.0
    ).astype(bf16)
    for g in range(groups):
        blend[g] = dot(mix_ref[g], place, TN).astype(bf16)

    stencil = band[:, 0 : span * ext]

    def column(c):
        x = xs[pl.ds(c, ext, stride=channels), :]
        h = hs[pl.ds(c, ext, stride=channels), :]
        pieces = []
        for s in range(-rim, rim + 1):
            if s == 0:
                pieces.append(x)
                continue
            inside = (lane + s >= 0) & (lane + s < cols)
            shift = (-s) % cols
            pieces.append(
                jnp.where(inside, pltpu.roll(x, shift, 1), pltpu.roll(h, shift, 1))
            )
        return jnp.concatenate([p.astype(bf16) for p in pieces], axis=0)

    for g in range(groups):

        def pair(number, carry):
            c = g * width + 2 * number
            both = jnp.concatenate([column(c), column(c + 1)], axis=1)
            r = dot(stencil, both).astype(bf16)
            at = pl.multiple_of(number * 2 * k_pad, k_pad)
            resp[:, pl.ds(at, k_pad), :] = r[:, 0:cols].reshape(rows, k_pad, cols)
            resp[:, pl.ds(at + k_pad, k_pad), :] = r[:, cols:].reshape(rows, k_pad, cols)
            return carry

        lax.fori_loop(0, width // 2, pair, 0, unroll=8)
        for i in range(0, rows, 2):
            operand = jnp.concatenate([resp[i], resp[i + 1]], axis=1)
            out = dot(blend[g], operand)
            emit(g, i, out[:, 0:cols])
            emit(g, i + 1, out[:, cols:])


def forward_kernel(*refs):
    act_ref, slope_ref = refs[8:10]
    width = refs[7].shape[2]
    chans = act_ref.shape[2]
    root = math.sqrt(2.0 / math.pi)

    def emit(g, i, v):
        square = v * v
        t = jnp.tanh(root * v * (1.0 + 0.044715 * square))
        half = 0.5 * (1.0 + t)
        act = v * half
        slope_ref[i, g * width : (g + 1) * width, :] = half + 0.5 * v * (1.0 - t * t) * (
            root + (root * 3.0 * 0.044715) * square
        )
        for j in range(width // chans):
            act_ref[g * (width // chans) + j, i] = act[j * chans : (j + 1) * chans, :].astype(bf16)

    conv_body(*refs[:8], *refs[10:], emit)


def adjoint_kernel(*refs):
    cot_ref, grad_ref = refs[8:10]
    width = refs[7].shape[2]

    def emit(g, i, v):
        at = slice(g * width, (g + 1) * width)
        grad_ref[i, at, :] = (cot_ref[i, at, :].astype(f32) + v).astype(bf16)

    conv_body(*refs[:8], *refs[10:], emit)


def conv_call(kernel, name, where, x, halo, stencil, mix, extra, outs):
    rows, channels, cols = x.shape
    groups, _, width = mix.shape
    ins = (where, x, *halo, stencil, mix, *extra)
    rim = stencil.shape[1] // 10
    flat = (rows + 2 * rim) * channels
    return pl.pallas_call(
        kernel,
        out_shape=outs,
        in_specs=[pl.BlockSpec(memory_space=pltpu.SMEM)] + vmem(len(ins) - 1),
        out_specs=tuple(vmem(len(outs))),
        scratch_shapes=[
            pltpu.VMEM((flat, cols), f32),
            pltpu.VMEM((flat, cols), f32),
            pltpu.VMEM((rows, width * 16, cols), bf16),
            pltpu.VMEM((rows * 16, 128), bf16),
            pltpu.VMEM((groups, width, width * 16), bf16),
        ],
        compiler_params=params(),
        cost_estimate=cost(1.2e10, 4e6),
        name=name,
    )(*ins)


def shifted(axis, step):
    count = lax.axis_size(axis)
    return [(a, (a + step) % count) for a in range(count)]


def lat_rims(x, left, right, rim):
    rows, channels, cols = x.shape
    low = jnp.concatenate([x[-rim:].reshape(rim * channels, cols), left[-8:], right[-8:]], axis=0)
    high = jnp.concatenate([x[:rim].reshape(rim * channels, cols), left[:8], right[:8]], axis=0)
    low = lax.ppermute(low, "lat", shifted("lat", 1))
    high = lax.ppermute(high, "lat", shifted("lat", -1))
    return low, high, left, right


def slope_kernel(edge, act_ref, slope_ref, out_ref, left_ref, right_ref):
    blocks, rows, chans, cols = act_ref.shape
    channels = blocks * chans

    def one(i, carry):
        parts = [act_ref[b, i].astype(f32) for b in range(blocks)]
        out_ref[i] = (slope_ref[i] * jnp.concatenate(parts, axis=0)).astype(bf16)
        return carry

    lax.fori_loop(0, rows, one, 0)
    first, last = edge_blocks(out_ref[...].reshape(rows * channels, cols), edge)
    left_ref[...] = first.astype(bf16)
    right_ref[...] = last.astype(bf16)


def slope_step(cot_act, slope, edge):
    rows, channels, cols = slope.shape
    blocks = len(chunk_blocks(rows * channels // 128, edge))
    shape = jax.ShapeDtypeStruct((8 * blocks, cols), bf16)
    return pl.pallas_call(
        functools.partial(slope_kernel, edge),
        out_shape=(jax.ShapeDtypeStruct(slope.shape, bf16), shape, shape),
        in_specs=vmem(2),
        out_specs=tuple(vmem(3)),
        compiler_params=params(),
        cost_estimate=cost(1e8, 3e6),
        name="slope_step",
    )(cot_act, slope)


def stencil_rows(weights):
    rows, span, _, k_count = weights.shape
    w = jnp.transpose(weights, (0, 3, 2, 1)).reshape(rows, k_count, span * span)
    w = jnp.pad(w, ((0, 0), (0, 16 - k_count), (0, 0)))
    return w.reshape(rows * 16, span * span).astype(bf16)


def local(input_field, basis_values, support_reach, mix_weight, filter_weight, cotangent):
    _, rows, channels, cols = input_field.shape
    rim = basis_values.shape[1] // 2
    degrees = filter_weight.shape[0]
    groups, k_count, width, _ = mix_weight.shape
    lat_count = lax.axis_size("lat")
    lon_count = lax.axis_size("lon")
    nlat = rows * lat_count
    nlon = cols * lon_count
    lat_index = lax.axis_index("lat")
    lon_index = lax.axis_index("lon")
    m_count = degrees // lat_count
    chans = channels // lon_count
    row_start = lat_index * rows
    field = input_field[0]
    cot = cotangent[0]

    edge = rim * channels // 128
    body = rows * chans

    sent = start_step(lon_index, cot, field, lon_count, edge)
    circ_c = lax.all_to_all(sent, "lon", 0, 0, tiled=True)

    blocks = 8 * len(chunk_blocks(rows * channels // 128, edge))
    strips = circ_c[:, body : body + blocks]
    left = lax.dynamic_index_in_dim(strips, (lon_index + lon_count - 1) % lon_count, 0, False)
    right = lax.dynamic_index_in_dim(strips, (lon_index + 1) % lon_count, 0, False)
    halo = lat_rims(field, left, right, rim)
    offsets = jnp.abs(jnp.arange(2 * rim + 1, dtype=jnp.int32) - rim)
    pad = ((rim, rim), (0, 0), (0, 0), (0, 0))
    basis_ext = lax.dynamic_slice_in_dim(jnp.pad(basis_values, pad), row_start, rows + 2 * rim, 0)
    reach_ext = lax.dynamic_slice_in_dim(
        jnp.pad(support_reach, pad[:2]), row_start, rows + 2 * rim, 0
    )
    inside = offsets[None, None, :] <= reach_ext[:, :, None]
    weights_ext = jnp.where(inside[..., None], basis_ext, 0.0)
    stencil = stencil_rows(weights_ext[rim : rim + rows])
    span = 2 * rim + 1
    flipped = jnp.stack(
        [weights_ext[a : a + rows, span - 1 - a, ::-1, :] for a in range(span)], axis=1
    )
    stencil_adj = stencil_rows(flipped)
    mix = mix_weight.reshape(groups, k_count * width, width)
    mix_adj = jnp.transpose(mix_weight, (0, 1, 3, 2)).reshape(groups, k_count * width, width)
    where = jnp.stack([lat_index, jnp.int32(nlat)]).astype(jnp.int32)
    act, slope = conv_call(
        forward_kernel,
        "conv_forward",
        where,
        field,
        halo,
        stencil,
        mix,
        (),
        (
            jax.ShapeDtypeStruct((lon_count, rows, chans, cols), bf16),
            jax.ShapeDtypeStruct((rows, channels, cols), f32),
        ),
    )

    tab = lon_table(degrees, nlon, lat_count)
    table, flip = legendre_tables(lat_index, degrees, lat_count, rows, m_count)
    theta = math.pi * (np.arange(nlat) + 0.5) / nlat
    quad = 2.0 * math.pi * math.pi / nlat * np.sin(theta) / nlon
    quad_rows = np.repeat(quad.reshape(lat_count, rows), chans, axis=1).astype(np.float32)
    quad_lanes = lax.dynamic_slice_in_dim(jnp.asarray(quad_rows), lat_index, 1, 0)
    post = np.broadcast_to(quad.reshape(lat_count, rows).T.reshape(nlat, 1), (nlat, 128))
    gains = lax.dynamic_slice_in_dim(filter_weight, lon_index * chans, chans, 1)
    gains = jnp.pad(jnp.concatenate([gains] * 2, axis=1), ((0, 0), (0, 128 - 2 * chans)))

    post = jnp.asarray(post.astype(np.float32))
    shape = (lon_count, rows, chans, cols)
    send_1 = analysis(circ_c, body, tab, quad_lanes, lat_count, True)
    recv_1 = lax.all_to_all(send_1, "lat", 0, 0, tiled=True)
    recv_1, act = lax.optimization_barrier((recv_1, act))
    circ_f = lax.all_to_all(act, "lon", 0, 0, tiled=True)
    filtered_c = filter_step(lat_index, recv_1, table, flip, gains, post, chans, True)
    send_2 = analysis(circ_f, body, tab, quad_lanes, lat_count, False, (filtered_c,))
    recv_2 = lax.all_to_all(send_2, "lat", 0, 0, tiled=True)
    cot_act = lax.all_to_all(synthesis(recv_2, tab, 1, shape), "lon", 0, 0, tiled=True)
    filtered_f = filter_step(lat_index, recv_2, table, flip, gains, post, chans, False)
    cot_act, filtered_f = lax.optimization_barrier((cot_act, filtered_f))
    recv_3 = lax.all_to_all(filtered_f, "lat", 0, 0, tiled=True)
    branch = lax.all_to_all(synthesis(recv_3, tab, 0, shape), "lon", 0, 0, tiled=True)

    cot_conv, first_c, last_c = slope_step(cot_act, slope, edge)
    left_c = lax.ppermute(last_c, "lon", shifted("lon", 1))
    right_c = lax.ppermute(first_c, "lon", shifted("lon", -1))
    (grad_field,) = conv_call(
        adjoint_kernel,
        "conv_adjoint",
        where,
        cot_conv,
        lat_rims(cot_conv, left_c, right_c, rim),
        stencil_adj,
        mix_adj,
        (cot,),
        (jax.ShapeDtypeStruct((rows, channels, cols), bf16),),
    )
    branch = jnp.transpose(branch, (1, 0, 2, 3)).reshape(rows, channels, cols)
    block_out = (field.astype(f32) + branch.astype(f32)).astype(bf16)
    return block_out[None], grad_field[None]


def solution(mesh):
    placed = (P(None, "lat", None, "lon"), P(), P(), P(), P(), P(None, "lat", None, "lon"))
    return jax.shard_map(
        local,
        mesh=mesh,
        in_specs=placed,
        out_specs=(P(None, "lat", None, "lon"), P(None, "lat", None, "lon")),
        check_vma=False,
    )
```

```python
import functools
import math

import jax
import jax.numpy as jnp
import numpy as np
from jax import lax
from jax.experimental import pallas as pl
from jax.experimental.pallas import tpu as pltpu
from jax.sharding import PartitionSpec as P

huge_value = 2.0**60
tiny_value = 2.0 ** (-60)
log_step = 41.58883083359672

f32 = jnp.float32
bf16 = jnp.bfloat16

NT = (((1,), (1,)), ((), ()))
NN = (((1,), (0,)), ((), ()))
TN = (((0,), (0,)), ((), ()))


def dot(a, b, dims=NN):
    return lax.dot_general(a, b, dims, preferred_element_type=f32)


def params(mib=20):
    return pltpu.CompilerParams(vmem_limit_bytes=mib * 1024 * 1024)


def vmem(count):
    return [pl.BlockSpec(memory_space=pltpu.VMEM)] * count


def hbm(count):
    return [pl.BlockSpec(memory_space=pl.ANY)] * count


def cost(flops, nbytes):
    return pl.CostEstimate(flops=int(flops), bytes_accessed=int(nbytes), transcendentals=0)


def legendre_fill(
    m_count, idx_ref, rise_ref, fall_ref, norm_ref, cos_ref, logsin_ref, keep, table_ref, flip_ref,
    table_out, flip_out, sems
):
    m_pad, lat = norm_ref.shape[0], cos_ref.shape[1]
    degrees = table_ref.shape[1]
    wide = lat // 128
    first = idx_ref[0] * m_count
    order = first + lax.broadcasted_iota(jnp.int32, (m_pad, 128), 0)
    order_real = order.astype(f32)
    square = order_real * order_real
    cosine = [
        jnp.broadcast_to(cos_ref[:, p * 128 : (p + 1) * 128], (m_pad, 128)) for p in range(wide)
    ]
    base = [
        norm_ref[...] + order_real * logsin_ref[:, p * 128 : (p + 1) * 128] for p in range(wide)
    ]

    def block(number, carry):
        latest, earlier, exponent, gain_b = carry
        latest, earlier, exponent = list(latest), list(earlier), list(exponent)
        for step in range(16):
            degree = number * 16 + step
            if step % 4 == 0:
                scale = []
                for p in range(wide):
                    grown = jnp.abs(latest[p]) > huge_value
                    latest[p] = jnp.where(grown, latest[p] * tiny_value, latest[p])
                    earlier[p] = jnp.where(grown, earlier[p] * tiny_value, earlier[p])
                    exponent[p] = jnp.where(grown, exponent[p] + 1.0, exponent[p])
                    scale.append(jnp.exp(base[p] + exponent[p] * log_step))
            d = degree.astype(f32)
            width = d * d - square
            inverse = lax.rsqrt(jnp.maximum(width, 1.0))
            gain_a = rise_ref[degree] * inverse
            both = gain_a * gain_b
            start_here = order == degree
            for p in range(wide):
                fresh = (gain_a * cosine[p]) * latest[p] - both * earlier[p]
                fresh = jnp.where(start_here, 1.0, fresh)
                earlier[p] = latest[p]
                latest[p] = fresh
                keep[p, step * m_pad : (step + 1) * m_pad, :] = fresh * scale[p]
            gain_b = fall_ref[degree] * (jnp.maximum(width, 0.0) * inverse)
        for m in range(m_count):
            rows = jnp.concatenate(
                [keep[part, pl.ds(m, 16, stride=m_pad), :] for part in range(wide)], axis=1
            )
            table_ref[m, pl.ds(pl.multiple_of(number * 16, 16), 16), :] = rows.astype(bf16)
        return tuple(latest), tuple(earlier), tuple(exponent), gain_b

    zero = jnp.zeros((m_pad, 128), f32)
    zeros = (zero,) * wide
    lax.fori_loop(0, degrees // 16, block, (zeros, zeros, zeros, zero))

    def turn(m, carry):
        pltpu.make_async_copy(table_ref.at[m], table_out.at[m], sems.at[0, m]).start()
        flip_ref[m] = jnp.transpose(table_ref[m])
        pltpu.make_async_copy(flip_ref.at[m], flip_out.at[m], sems.at[1, m]).start()
        return carry

    lax.fori_loop(0, m_count, turn, 0)


def legendre_inputs(lat_index, degrees, lat_count, row_count, m_count):
    nlat = lat_count * row_count
    m_pad = 16
    place = np.arange(nlat)
    t = (place % lat_count) * row_count + place // lat_count
    theta = math.pi * (t + 0.5) / nlat
    counter = np.arange(1, degrees, dtype=np.float64)
    running = np.concatenate([[0.0], np.cumsum(np.log((2 * counter - 1) / (2 * counter)))])
    m = np.arange(degrees)
    norm = 0.5 * np.log((2 * m + 1) / (4 * math.pi)) + 0.5 * running
    norms = np.zeros((lat_count, m_pad, 1), np.float32)
    norms[:, :m_count, 0] = norm.reshape(lat_count, m_count)
    norm_mine = lax.dynamic_index_in_dim(jnp.asarray(norms), lat_index, 0, keepdims=False)
    rise = np.sqrt(np.maximum(4.0 * m * m - 1.0, 1.0)).astype(np.float32)
    fall = (1.0 / np.sqrt(np.maximum(4.0 * m * m - 1.0, 1.0))).astype(np.float32)
    return (
        jnp.asarray(rise),
        jnp.asarray(fall),
        norm_mine,
        jnp.asarray(np.cos(theta)[None].astype(np.float32)),
        jnp.asarray(np.log(np.sin(theta))[None].astype(np.float32)),
    )


def lon_kernel(near_cos_ref, near_sin_ref, far_ref, tab_ref):
    blocks = tab_ref.shape[1] // 128
    for b in range(blocks):
        tab_ref[:, b * 128 : (b + 1) * 128] = (
            near_cos_ref[...] * far_ref[:, b : b + 1]
            - near_sin_ref[...] * far_ref[:, blocks + b : blocks + b + 1]
        ).astype(bf16)


def lon_table(degrees, nlon, owners):
    per = degrees // owners
    row = np.arange(2 * degrees)
    m_np = row // (2 * per) * per + row % per
    m = jnp.asarray(m_np.astype(np.int32))
    shift = jnp.asarray(((row // per % 2) * (nlon // 4)).astype(np.int32))
    low = jnp.arange(128, dtype=jnp.int32)
    angle = (m[:, None] * low[None, :] + shift[:, None]) % nlon
    phase = 2.0 * math.pi / nlon * angle.astype(f32)
    far = 2.0 * math.pi * ((m_np[:, None] * np.arange(nlon // 128)[None] * 128) % nlon) / nlon
    far = np.concatenate([np.cos(far), np.sin(far)], axis=1).astype(np.float32)
    return pl.pallas_call(
        lon_kernel,
        out_shape=jax.ShapeDtypeStruct((2 * degrees, nlon), bf16),
        in_specs=vmem(3),
        out_specs=vmem(1)[0],
        compiler_params=params(),
        cost_estimate=cost(1e8, 3e6),
        name="lon_table",
    )(jnp.cos(phase), jnp.sin(phase), jnp.asarray(far))


def pack_rows(z, k_count):
    third = k_count // 3
    rest = [z[j * third : (j + 1) * third, 256:288] for j in range(3)]
    rest.append(jnp.zeros((third, 32), f32))
    return jnp.concatenate([z[:, 0:128], z[:, 128:256], jnp.concatenate(rest, axis=1)], axis=0)


def analysis_kernel(k_count, cotangent_pass, *refs):
    circ_ref, tab_ref, quad_ref = refs[:3]
    out_ref, keep = refs[-2:]
    sectors = circ_ref.shape[0]
    lines = keep.shape[1]
    owners = out_ref.shape[0]
    height = 2 * k_count + k_count // 3
    if len(circ_ref.shape) == 3:
        parts = [circ_ref[s, 0:lines, :] for s in range(sectors)]
    else:
        parts = [circ_ref[s].astype(f32).reshape(lines, -1).astype(bf16) for s in range(sectors)]
    circ = jnp.concatenate(parts, axis=1)
    z = dot(tab_ref[...], circ, NT)
    if cotangent_pass:
        row = lax.broadcasted_iota(jnp.int32, z.shape, 0)
        z = z * jnp.where((row == 0) | (row == k_count // 2), 1.0, 2.0)
    else:
        z = z * quad_ref[...]
    keep[...] = z
    for e in range(owners):
        piece = keep[e * k_count : (e + 1) * k_count, :]
        out_ref[e, 0:height, :] = pack_rows(piece, k_count).astype(bf16)
        if len(refs) > 5:
            out_ref[e, height:, :] = refs[3][e]


def analysis(circ, lines, tab, quad_lanes, owners, cotangent_pass, beside=()):
    k_count = tab.shape[0] // owners
    height = (2 * k_count + k_count // 3) * (1 + len(beside))
    return pl.pallas_call(
        functools.partial(analysis_kernel, k_count, cotangent_pass),
        out_shape=jax.ShapeDtypeStruct((owners, height, 128), bf16),
        in_specs=vmem(3 + len(beside)),
        out_specs=vmem(1)[0],
        scratch_shapes=[pltpu.VMEM((tab.shape[0], lines), f32)],
        compiler_params=params(),
        cost_estimate=cost(2 * tab.shape[0] * tab.shape[1] * lines, 3e6),
        name="analysis",
    )(circ, tab, quad_lanes, *beside)


def filter_body(
    m_count, chans, cotangent_pass, idx_ref, recv_ref, weight_ref, post_ref, out_ref,
    took, give, gain, table_ref, flip_ref, ready
):
    places, height, _ = out_ref.shape
    k_count = 2 * m_count
    third = k_count // 3
    nlat = table_ref.shape[1]
    rows = nlat // places
    lane = lax.broadcasted_iota(jnp.int32, (places, 128), 1)

    def load(d, carry):
        at = pl.ds(pl.multiple_of(d * height, 8), height)
        took[at, :] = recv_ref[d, 0:height, :].astype(f32)
        return carry

    lax.fori_loop(0, places, load, 0, unroll=4)
    give[2 * k_count * places :, :] = jnp.zeros((third * places, 128), f32)
    weight = weight_ref[...]
    room = 256 - weight.shape[1]
    weight = jnp.concatenate([weight, jnp.zeros((weight.shape[0], room), f32)], axis=1)
    weight = pltpu.roll(weight, lax.rem(256 - idx_ref[1] * chans, 256), 1)[:, 0:128]
    place = lax.broadcasted_iota(jnp.int32, weight.shape, 1)
    weight = jnp.where(place < chans, weight, 0.0)
    gain[...] = weight + pltpu.roll(weight, chans, 1)

    def one(mm):
        blocks = []
        for r in range(2):
            k = r * m_count + mm
            b0 = took[pl.ds(k, places, stride=height), :]
            b1 = took[pl.ds(k_count + k, places, stride=height), :]
            b2 = took[pl.ds(2 * k_count + k % third, places, stride=height), :]
            b2 = pltpu.roll(b2, (128 - 32 * (k // third)) % 128, 1)
            blocks.append((b0, b1, b2))
        columns = []
        for i in range(rows):
            start = i * chans
            first, last = start // 128, (start + chans - 1) // 128
            total = None
            for q, b in enumerate(blocks):
                if first == last:
                    source = b[first]
                else:
                    source = jnp.where(lane < 64, b[last], b[first])
                shift = (q * chans - start) % 128
                source = pltpu.roll(source, shift, 1) if shift else source
                total = source if total is None else jnp.where(lane < chans, total, source)
            columns.append(total)
        x = jnp.concatenate(columns, axis=0).astype(bf16)
        coeffs = dot(table_ref[mm], x)
        filtered = (coeffs * gain[...]).astype(bf16)
        y = dot(flip_ref[mm], filtered)
        if cotangent_pass:
            y = y * post_ref[...]
        else:
            y = y * jnp.where(idx_ref[0] * m_count + mm == 0, 1.0, 2.0).astype(f32)
        for r in range(2):
            k = r * m_count + mm
            outs = [jnp.zeros((places, 128), f32) for _ in range(3)]
            for i in range(rows):
                start = i * chans
                first, last = start // 128, (start + chans - 1) // 128
                shift = (start - r * chans) % 128
                piece = y[i * places : (i + 1) * places, :]
                piece = pltpu.roll(piece, shift, 1) if shift else piece
                for part in range(first, last + 1):
                    lo, hi = start - part * 128, start + chans - part * 128
                    outs[part] = jnp.where((lane >= lo) & (lane < hi), piece, outs[part])
            give[pl.ds(k * places, places), :] = outs[0]
            give[pl.ds((k_count + k) * places, places), :] = outs[1]
            at = pl.ds((2 * k_count + k % third) * places, places)
            give[at, :] = give[at, :] + pltpu.roll(outs[2], 32 * (k // third), 1)

    def group(number, carry):
        for m in range(3):
            ready(number * 3 + m)
        for m in range(3):
            one(number * 3 + m)
        return carry

    lax.fori_loop(0, m_count // 3, group, 0)

    def store(d, carry):
        out_ref[d] = give[pl.ds(d, height, stride=places), :].astype(bf16)
        return carry

    lax.fori_loop(0, places, store, 0, unroll=4)


def legendre_kernel(
    m_count, idx_ref, rise_ref, fall_ref, norm_ref, cos_ref, logsin_ref, table_out, flip_out,
    keep, table, flip, sems
):
    legendre_fill(
        m_count, idx_ref, rise_ref, fall_ref, norm_ref, cos_ref, logsin_ref, keep, table, flip,
        table_out, flip_out, sems,
    )

    def finish(m, carry):
        pltpu.make_async_copy(table.at[m], table_out.at[m], sems.at[0, m]).wait()
        pltpu.make_async_copy(flip.at[m], flip_out.at[m], sems.at[1, m]).wait()
        return carry

    lax.fori_loop(0, m_count, finish, 0)


def legendre_tables(where, legendre, m_count, degrees, nlat):
    smem = pl.BlockSpec(memory_space=pltpu.SMEM)
    return pl.pallas_call(
        functools.partial(legendre_kernel, m_count),
        out_shape=(
            jax.ShapeDtypeStruct((m_count, degrees, nlat), bf16),
            jax.ShapeDtypeStruct((m_count, nlat, degrees), bf16),
        ),
        in_specs=[smem] * 3 + vmem(3),
        out_specs=tuple(hbm(2)),
        scratch_shapes=[
            pltpu.VMEM((nlat // 128, 16 * 16, 128), f32),
            *table_scratch(m_count, degrees, nlat),
        ],
        compiler_params=params(60),
        cost_estimate=cost(2e9, 7e6),
        name="legendre_tables",
    )(where, *legendre)


def filter_kernel(
    m_count, chans, cotangent_pass, idx_ref, recv_ref, weight_ref, post_ref, table_in, flip_in,
    out_ref, took, give, gain, table, flip, sems
):
    def begin(m, carry):
        pltpu.make_async_copy(table_in.at[m], table.at[m], sems.at[0, m]).start()
        pltpu.make_async_copy(flip_in.at[m], flip.at[m], sems.at[1, m]).start()
        return carry

    lax.fori_loop(0, m_count, begin, 0)

    def ready(m):
        pltpu.make_async_copy(table_in.at[m], table.at[m], sems.at[0, m]).wait()
        pltpu.make_async_copy(flip_in.at[m], flip.at[m], sems.at[1, m]).wait()

    filter_body(
        m_count, chans, cotangent_pass, idx_ref, recv_ref, weight_ref, post_ref, out_ref,
        took, give, gain, table, flip, ready,
    )


def filter_scratch(places, height, degrees):
    return [
        pltpu.VMEM((places * height, 128), f32),
        pltpu.VMEM((places * height, 128), f32),
        pltpu.VMEM((degrees, 128), f32),
    ]


def table_scratch(m_count, degrees, nlat):
    return [
        pltpu.VMEM((m_count, degrees, nlat), bf16),
        pltpu.VMEM((m_count, nlat, degrees), bf16),
        pltpu.SemaphoreType.DMA((2, m_count)),
    ]


def filter_step(where, recv, weight, post, table, flip, chans, cotangent_pass):
    places = recv.shape[0]
    m_count, degrees, nlat = table.shape
    height = 4 * m_count + 2 * m_count // 3
    return pl.pallas_call(
        functools.partial(filter_kernel, m_count, chans, cotangent_pass),
        out_shape=jax.ShapeDtypeStruct((places, height, 128), bf16),
        in_specs=[pl.BlockSpec(memory_space=pltpu.SMEM)] + vmem(3) + hbm(2),
        out_specs=vmem(1)[0],
        scratch_shapes=[
            *filter_scratch(places, height, degrees),
            *table_scratch(m_count, degrees, nlat),
        ],
        compiler_params=params(60),
        cost_estimate=cost(8e9, 9e6),
        name="filter_step",
    )(where, recv, weight, post, table, flip)


def synthesis_kernel(which, recv_ref, tab_ref, out_ref):
    owners = recv_ref.shape[0]
    k_count = tab_ref.shape[0] // owners
    height = 2 * k_count + k_count // 3
    sectors, rows, chans, cols = out_ref.shape
    left, middle, right = [], [], []
    for e in range(owners):
        v = recv_ref[e, which * height : (which + 1) * height, :].astype(f32)
        left.append(v[0:k_count])
        middle.append(v[k_count : 2 * k_count])
        rest = v[2 * k_count :]
        for j in range(3):
            right.append(pltpu.roll(rest, (128 - 32 * j) % 128, 1) if j else rest)
    flat = [jnp.transpose(jnp.concatenate(part, axis=0)) for part in (left, middle, right)]
    s = jnp.concatenate([flat[0], flat[1], flat[2][0:32]], axis=0).astype(bf16)
    circ = dot(s, tab_ref[...])
    for sector in range(sectors):
        piece = circ[:, sector * cols : (sector + 1) * cols]
        out_ref[sector] = piece.reshape(rows, chans, cols).astype(bf16)


def synthesis(recv, tab, which, shape):
    return pl.pallas_call(
        functools.partial(synthesis_kernel, which),
        out_shape=jax.ShapeDtypeStruct(shape, bf16),
        in_specs=vmem(2),
        out_specs=vmem(1)[0],
        compiler_params=params(),
        cost_estimate=cost(2 * tab.shape[0] * tab.shape[1] * shape[1] * shape[2], 5e6),
        name="synthesis",
    )(recv, tab)


def chunk_blocks(count, edge):
    inner = list(range(edge, count - edge))
    return (
        [list(range(edge))]
        + [inner[k : k + 4] for k in range(0, len(inner), 4)]
        + [list(range(count - edge, count))]
    )


def edge_blocks(flat, edge):
    row = lax.broadcasted_iota(jnp.int32, (16, 128), 0)
    lane = lax.broadcasted_iota(jnp.int32, (16, 128), 1)
    first = []
    last = []
    for chunks in chunk_blocks(flat.shape[0] // 128, edge):
        total = jnp.zeros((16, 128), f32)
        for v, chunk in enumerate(chunks):
            head = (row == 2 * v + lane) & (lane < 2)
            tail = (row - 8 - 2 * v == lane - 126) & (lane >= 126)
            select = jnp.where(head | tail, 1.0, 0.0).astype(bf16)
            total = total + dot(select, flat[chunk * 128 : (chunk + 1) * 128], NT)
        first.append(total[0:8])
        last.append(total[8:16])
    return jnp.concatenate(first, axis=0), jnp.concatenate(last, axis=0)


def start_kernel(edge, idx_ref, cot_ref, field_ref, out_ref):
    sectors, height, cols = out_ref.shape
    rows, channels, _ = cot_ref.shape
    chans = channels // sectors
    body = rows * chans
    field = field_ref[...].reshape(rows * channels, cols)
    first, last = edge_blocks(field, edge)
    for b in range(sectors):
        parts = [cot_ref[i, b * chans : (b + 1) * chans, :].astype(f32) for i in range(rows)]
        right = lax.rem(idx_ref[0] + 1, sectors) == b
        parts.append(jnp.where(right, last, first))
        room = height - body - first.shape[0]
        parts.append(jnp.zeros((room, cols), f32))
        out_ref[b] = jnp.concatenate(parts, axis=0).astype(bf16)


def start_step(lon_index, cot, field, sectors, edge):
    rows, channels, cols = cot.shape
    body = rows * channels // sectors
    blocks = len(chunk_blocks(rows * channels // 128, edge))
    height = -(-(body + 8 * blocks) // 16) * 16
    return pl.pallas_call(
        functools.partial(start_kernel, edge),
        out_shape=jax.ShapeDtypeStruct((sectors, height, cols), bf16),
        in_specs=[pl.BlockSpec(memory_space=pltpu.SMEM)] + vmem(2),
        out_specs=vmem(1)[0],
        compiler_params=params(),
        cost_estimate=cost(1e8, 2e6),
        name="start",
    )(lon_index[None], cot, field)


def weights_kernel(rim, adjoint, idx_ref, stencil_ref, mix_ref, band, blend):
    groups, width = mix_ref.shape[0], mix_ref.shape[2]
    taps = mix_ref.shape[1] // width
    k_pad = 16
    ext = stencil_ref.shape[0] // k_pad
    rows = ext - 2 * rim
    span = 2 * rim + 1

    tap = lax.broadcasted_iota(jnp.int32, (span * span, 128), 0)
    slot = lax.broadcasted_iota(jnp.int32, (span * span, 128), 1)
    source = idx_ref[0] * rows - rim + slot % ext
    inside = (source >= 0) & (source < idx_ref[1]) & (slot < span * ext)
    for i in range(rows):
        total = jnp.zeros((k_pad, 128), f32)
        for line in range(i, i + span) if adjoint else (i + rim,):
            if adjoint:
                hit = (span - 1 - tap // span == slot // ext) & (slot % ext == line)
                hit = hit & (tap % span == i - line + span - 1)
            else:
                hit = (tap // span == slot // ext) & (slot % ext == i + tap % span)
            place = jnp.where(inside & hit, 1.0, 0.0).astype(bf16)
            total = total + dot(stencil_ref[line * k_pad : (line + 1) * k_pad, :], place)
        band[i * k_pad : (i + 1) * k_pad, :] = total.astype(bf16)

    depth = width * k_pad
    pair_row = lax.broadcasted_iota(jnp.int32, (taps * width, depth), 0)
    pair_lane = lax.broadcasted_iota(jnp.int32, (taps * width, depth), 1)
    place = jnp.where(
        pair_lane == (pair_row % width) * k_pad + pair_row // width, 1.0, 0.0
    ).astype(bf16)
    for g in range(groups):
        blend[g] = dot(mix_ref[g], place, TN).astype(bf16)


def conv_weights(where, stencil, mix, rim, adjoint):
    groups, _, width = mix.shape
    return pl.pallas_call(
        functools.partial(weights_kernel, rim, adjoint),
        out_shape=(
            jax.ShapeDtypeStruct((stencil.shape[0] - 32 * rim, 128), bf16),
            jax.ShapeDtypeStruct((groups, width, width * 16), bf16),
        ),
        in_specs=[pl.BlockSpec(memory_space=pltpu.SMEM)] + vmem(2),
        out_specs=tuple(vmem(2)),
        compiler_params=params(),
        cost_estimate=cost(4e8, 1e6),
        name="conv_weights",
    )(where, stencil, mix)


def conv_body(
    x_ref, low_ref, high_ref, left_ref, right_ref, band_ref, blend_ref, xs, hs, resp, emit
):
    rows, channels, cols = x_ref.shape
    groups, width, _ = blend_ref.shape
    ext = hs.shape[0] // channels
    rim = (ext - rows) // 2
    span = 2 * rim + 1
    edge = rim * channels // 128
    k_pad = 16
    xs[0 : rim * channels, :] = low_ref[0 : rim * channels].astype(f32)
    xs[rim * channels : (rim + rows) * channels, :] = (
        x_ref[...].astype(f32).reshape(rows * channels, cols)
    )
    xs[(rim + rows) * channels :, :] = high_ref[0 : rim * channels].astype(f32)

    row = lax.broadcasted_iota(jnp.int32, (16, cols), 0)
    lane = lax.broadcasted_iota(jnp.int32, (16, cols), 1)

    def spread(left, right, chunks, base):
        turned = jnp.transpose(jnp.concatenate([left.astype(f32), right.astype(f32)], axis=0))
        turned = turned.astype(bf16)
        for v, chunk in enumerate(chunks):
            ahead = (row - 2 * v == lane - (cols - 2)) & (lane >= cols - 2)
            behind = (row - 8 - 2 * v == lane) & (lane < 2)
            put = jnp.where(ahead | behind, 1.0, 0.0).astype(bf16)
            at = (base + chunk) * 128
            hs[at : at + 128, :] = dot(turned, put)

    lists = chunk_blocks(rows * channels // 128, edge)
    tail = rim * channels
    spread(low_ref[tail : tail + 8], low_ref[tail + 8 : tail + 16], range(edge), 0)
    spread(high_ref[tail : tail + 8], high_ref[tail + 8 : tail + 16], range(edge),
           edge + rows * channels // 128)
    for u, chunks in enumerate(lists):
        at = slice(8 * u, 8 * u + 8)
        spread(left_ref[at], right_ref[at], chunks, edge)

    stencil = band_ref[:, 0 : span * ext]

    def column(c):
        x = xs[pl.ds(c, ext, stride=channels), :]
        h = hs[pl.ds(c, ext, stride=channels), :]
        pieces = []
        for s in range(-rim, rim + 1):
            if s == 0:
                pieces.append(x)
                continue
            inside = (lane + s >= 0) & (lane + s < cols)
            shift = (-s) % cols
            pieces.append(
                jnp.where(inside, pltpu.roll(x, shift, 1), pltpu.roll(h, shift, 1))
            )
        return jnp.concatenate([p.astype(bf16) for p in pieces], axis=0)

    for g in range(groups):

        def pair(number, carry):
            c = g * width + 2 * number
            both = jnp.concatenate([column(c), column(c + 1)], axis=1)
            r = dot(stencil, both).astype(bf16)
            at = pl.multiple_of(number * 2 * k_pad, k_pad)
            resp[:, pl.ds(at, k_pad), :] = r[:, 0:cols].reshape(rows, k_pad, cols)
            resp[:, pl.ds(at + k_pad, k_pad), :] = r[:, cols:].reshape(rows, k_pad, cols)
            return carry

        lax.fori_loop(0, width // 2, pair, 0, unroll=8)
        for i in range(0, rows, 2):
            operand = jnp.concatenate([resp[i], resp[i + 1]], axis=1)
            out = dot(blend_ref[g], operand)
            emit(g, i, out[:, 0:cols])
            emit(g, i + 1, out[:, cols:])


def forward_kernel(rim, *refs):
    where_ref, stencil_ref, mix_ref = refs[:3]
    act_ref, slope_ref, xs, hs, resp, band, blend = refs[8:]
    weights_kernel(rim, False, where_ref, stencil_ref, mix_ref, band, blend)
    width = blend.shape[1]
    chans = act_ref.shape[2]
    root = math.sqrt(2.0 / math.pi)

    def emit(g, i, v):
        square = v * v
        t = jnp.tanh(root * v * (1.0 + 0.044715 * square))
        half = 0.5 * (1.0 + t)
        act = v * half
        slope_ref[i, g * width : (g + 1) * width, :] = half + 0.5 * v * (1.0 - t * t) * (
            root + (root * 3.0 * 0.044715) * square
        )
        for j in range(width // chans):
            act_ref[g * (width // chans) + j, i] = act[j * chans : (j + 1) * chans, :].astype(bf16)

    conv_body(*refs[3:8], band, blend, xs, hs, resp, emit)


def adjoint_kernel(*refs):
    cot_ref, grad_ref = refs[7:9]
    width = refs[6].shape[1]

    def emit(g, i, v):
        at = slice(g * width, (g + 1) * width)
        grad_ref[i, at, :] = (cot_ref[i, at, :].astype(f32) + v).astype(bf16)

    conv_body(*refs[:7], *refs[9:], emit)


def conv_scratch(rim, x, width):
    rows, channels, cols = x.shape
    flat = (rows + 2 * rim) * channels
    return [
        pltpu.VMEM((flat, cols), f32),
        pltpu.VMEM((flat, cols), f32),
        pltpu.VMEM((rows, width * 16, cols), bf16),
    ]


def conv_forward(where, stencil, mix, rim, x, halo, shape):
    groups, _, width = mix.shape
    return pl.pallas_call(
        functools.partial(forward_kernel, rim),
        out_shape=(jax.ShapeDtypeStruct(shape, bf16), jax.ShapeDtypeStruct(x.shape, f32)),
        in_specs=[pl.BlockSpec(memory_space=pltpu.SMEM)] + vmem(7),
        out_specs=tuple(vmem(2)),
        scratch_shapes=[
            *conv_scratch(rim, x, width),
            pltpu.VMEM((x.shape[0] * 16, 128), bf16),
            pltpu.VMEM((groups, width, width * 16), bf16),
        ],
        compiler_params=params(),
        cost_estimate=cost(1.2e10, 4e6),
        name="conv_forward",
    )(where, stencil, mix, x, *halo)


def conv_adjoint(weights, rim, x, halo, cot):
    return pl.pallas_call(
        adjoint_kernel,
        out_shape=jax.ShapeDtypeStruct(x.shape, bf16),
        in_specs=vmem(8),
        out_specs=vmem(1)[0],
        scratch_shapes=conv_scratch(rim, x, weights[1].shape[1]),
        compiler_params=params(),
        cost_estimate=cost(1.2e10, 4e6),
        name="conv_adjoint",
    )(x, *halo, *weights, cot)


def shifted(axis, step):
    count = lax.axis_size(axis)
    return [(a, (a + step) % count) for a in range(count)]


def lat_rims(x, left, right, rim):
    rows, channels, cols = x.shape
    low = jnp.concatenate([x[-rim:].reshape(rim * channels, cols), left[-8:], right[-8:]], axis=0)
    high = jnp.concatenate([x[:rim].reshape(rim * channels, cols), left[:8], right[:8]], axis=0)
    low = lax.ppermute(low, "lat", shifted("lat", 1))
    high = lax.ppermute(high, "lat", shifted("lat", -1))
    return low, high, left, right


def slope_kernel(edge, act_ref, slope_ref, out_ref, left_ref, right_ref):
    blocks, rows, chans, cols = act_ref.shape
    channels = blocks * chans

    def one(i, carry):
        parts = [act_ref[b, i].astype(f32) for b in range(blocks)]
        out_ref[i] = (slope_ref[i] * jnp.concatenate(parts, axis=0)).astype(bf16)
        return carry

    lax.fori_loop(0, rows, one, 0)
    first, last = edge_blocks(out_ref[...].reshape(rows * channels, cols), edge)
    left_ref[...] = first.astype(bf16)
    right_ref[...] = last.astype(bf16)


def slope_step(cot_act, slope, edge):
    rows, channels, cols = slope.shape
    blocks = len(chunk_blocks(rows * channels // 128, edge))
    shape = jax.ShapeDtypeStruct((8 * blocks, cols), bf16)
    return pl.pallas_call(
        functools.partial(slope_kernel, edge),
        out_shape=(jax.ShapeDtypeStruct(slope.shape, bf16), shape, shape),
        in_specs=vmem(2),
        out_specs=tuple(vmem(3)),
        compiler_params=params(),
        cost_estimate=cost(1e8, 3e6),
        name="slope_step",
    )(cot_act, slope)


def stencil_rows(weights):
    rows, span, _, k_count = weights.shape
    w = jnp.transpose(weights, (0, 3, 2, 1)).reshape(rows, k_count, span * span)
    w = jnp.pad(w, ((0, 0), (0, 16 - k_count), (0, 0)))
    return w.reshape(rows * 16, span * span).astype(bf16)


def local(input_field, basis_values, support_reach, mix_weight, filter_weight, cotangent):
    _, rows, channels, cols = input_field.shape
    rim = basis_values.shape[1] // 2
    degrees = filter_weight.shape[0]
    groups, k_count, width, _ = mix_weight.shape
    lat_count = lax.axis_size("lat")
    lon_count = lax.axis_size("lon")
    nlat = rows * lat_count
    nlon = cols * lon_count
    lat_index = lax.axis_index("lat")
    lon_index = lax.axis_index("lon")
    m_count = degrees // lat_count
    chans = channels // lon_count
    row_start = lat_index * rows
    field = input_field[0]
    cot = cotangent[0]

    edge = rim * channels // 128
    body = rows * chans

    sent = start_step(lon_index, cot, field, lon_count, edge)
    circ_c = lax.all_to_all(sent, "lon", 0, 0, tiled=True)

    blocks = 8 * len(chunk_blocks(rows * channels // 128, edge))
    strips = circ_c[:, body : body + blocks]
    left = lax.dynamic_index_in_dim(strips, (lon_index + lon_count - 1) % lon_count, 0, False)
    right = lax.dynamic_index_in_dim(strips, (lon_index + 1) % lon_count, 0, False)
    offsets = jnp.abs(jnp.arange(2 * rim + 1, dtype=jnp.int32) - rim)
    pad = ((rim, rim), (0, 0), (0, 0), (0, 0))
    basis_ext = lax.dynamic_slice_in_dim(jnp.pad(basis_values, pad), row_start, rows + 2 * rim, 0)
    reach_ext = lax.dynamic_slice_in_dim(
        jnp.pad(support_reach, pad[:2]), row_start, rows + 2 * rim, 0
    )
    inside = offsets[None, None, :] <= reach_ext[:, :, None]
    weights_ext = jnp.where(inside[..., None], basis_ext, 0.0)
    stencil = stencil_rows(weights_ext)
    mix = mix_weight.reshape(groups, k_count * width, width)
    mix_adj = jnp.transpose(mix_weight, (0, 1, 3, 2)).reshape(groups, k_count * width, width)
    where = jnp.stack([lat_index, jnp.int32(nlat)]).astype(jnp.int32)
    tab = lon_table(degrees, nlon, lat_count)
    legendre = legendre_inputs(lat_index, degrees, lat_count, rows, m_count)
    theta = math.pi * (np.arange(nlat) + 0.5) / nlat
    quad = 2.0 * math.pi * math.pi / nlat * np.sin(theta) / nlon
    quad_rows = np.repeat(quad.reshape(lat_count, rows), chans, axis=1).astype(np.float32)
    quad_lanes = lax.dynamic_slice_in_dim(jnp.asarray(quad_rows), lat_index, 1, 0)
    post = np.broadcast_to(quad.reshape(lat_count, rows).T.reshape(nlat, 1), (nlat, 128))
    post = jnp.asarray(post.astype(np.float32))
    here = jnp.stack([lat_index, lon_index]).astype(jnp.int32)
    shape = (lon_count, rows, chans, cols)

    send_1 = analysis(circ_c, body, tab, quad_lanes, lat_count, True)
    halo = lat_rims(field, left, right, rim)
    send_1, halo = lax.optimization_barrier((send_1, halo))
    recv_1 = lax.all_to_all(send_1, "lat", 0, 0, tiled=True)
    act, slope = conv_forward(where, stencil, mix, rim, field, halo, shape)
    act, after = lax.optimization_barrier((act, here))
    table, flip = legendre_tables(after, legendre, m_count, degrees, nlat)
    recv_1, act, table, flip = lax.optimization_barrier((recv_1, act, table, flip))
    circ_f = lax.all_to_all(act, "lon", 0, 0, tiled=True)
    filtered_c = filter_step(here, recv_1, filter_weight, post, table, flip, chans, True)
    send_2 = analysis(circ_f, body, tab, quad_lanes, lat_count, False, (filtered_c,))
    recv_2 = lax.all_to_all(send_2, "lat", 0, 0, tiled=True)
    stencil, send_2 = lax.optimization_barrier((stencil, send_2))
    weights_adj = conv_weights(where, stencil, mix_adj, rim, True)
    recv_2, weights_adj = lax.optimization_barrier((recv_2, weights_adj))
    cot_act = lax.all_to_all(synthesis(recv_2, tab, 1, shape), "lon", 0, 0, tiled=True)
    filtered_f = filter_step(here, recv_2, filter_weight, post, table, flip, chans, False)
    recv_3 = lax.all_to_all(filtered_f, "lat", 0, 0, tiled=True)
    branch = lax.all_to_all(synthesis(recv_3, tab, 0, shape), "lon", 0, 0, tiled=True)

    cot_conv, first_c, last_c = slope_step(cot_act, slope, edge)
    left_c = lax.ppermute(last_c, "lon", shifted("lon", 1))
    right_c = lax.ppermute(first_c, "lon", shifted("lon", -1))
    halo_c = lat_rims(cot_conv, left_c, right_c, rim)
    grad_field = conv_adjoint(weights_adj, rim, cot_conv, halo_c, cot)
    branch = jnp.transpose(branch, (1, 0, 2, 3)).reshape(rows, channels, cols)
    block_out = (field.astype(f32) + branch.astype(f32)).astype(bf16)
    return block_out[None], grad_field[None]


def solution(mesh):
    placed = (P(None, "lat", None, "lon"), P(), P(), P(), P(), P(None, "lat", None, "lon"))
    return jax.shard_map(
        local,
        mesh=mesh,
        in_specs=placed,
        out_specs=(P(None, "lat", None, "lon"), P(None, "lat", None, "lon")),
        check_vma=False,
    )
```

```python
import functools
import math

import jax
import jax.numpy as jnp
import numpy as np
from jax import lax
from jax.experimental import pallas as pl
from jax.experimental.pallas import tpu as pltpu
from jax.sharding import PartitionSpec as P

huge_value = 2.0**60
tiny_value = 2.0 ** (-60)
log_step = 41.58883083359672

f32 = jnp.float32
bf16 = jnp.bfloat16

NT = (((1,), (1,)), ((), ()))
NN = (((1,), (0,)), ((), ()))
TN = (((0,), (0,)), ((), ()))


def dot(a, b, dims=NN):
    return lax.dot_general(a, b, dims, preferred_element_type=f32)


def params(mib=20):
    return pltpu.CompilerParams(vmem_limit_bytes=mib * 1024 * 1024)


def vmem(count):
    return [pl.BlockSpec(memory_space=pltpu.VMEM)] * count


def hbm(count):
    return [pl.BlockSpec(memory_space=pl.ANY)] * count


def cost(flops, nbytes):
    return pl.CostEstimate(flops=int(flops), bytes_accessed=int(nbytes), transcendentals=0)


def legendre_kernel(
    m_count, idx_ref, rise_ref, fall_ref, norm_ref, cos_ref, logsin_ref, table_out,
    keep, table_ref, sems
):
    m_pad, lat = 16, cos_ref.shape[1]
    degrees = table_ref.shape[1]
    wide = lat // 128
    first = idx_ref[0] * m_count
    order = first + lax.broadcasted_iota(jnp.int32, (m_pad, 128), 0)
    order_real = order.astype(f32)
    square = order_real * order_real
    cosine = [
        jnp.broadcast_to(cos_ref[:, p * 128 : (p + 1) * 128], (m_pad, 128)) for p in range(wide)
    ]
    local_row = lax.broadcasted_iota(jnp.int32, (m_pad, 128), 0)
    norm = jnp.zeros((m_pad, 128), f32)
    for m in range(m_count):
        norm = jnp.where(local_row == m, norm_ref[first + m], norm)
    base = [
        norm + order_real * logsin_ref[:, p * 128 : (p + 1) * 128] for p in range(wide)
    ]

    def copy_out(number):
        at = pl.ds(pl.multiple_of(number * 16, 16), 16)
        return pltpu.make_async_copy(table_ref.at[:, at], table_out.at[:, at], sems.at[number])

    def block(number, carry):
        latest, earlier, exponent, gain_b = carry
        latest, earlier, exponent = list(latest), list(earlier), list(exponent)
        for step in range(16):
            degree = number * 16 + step
            if step % 4 == 0:
                scale = []
                for p in range(wide):
                    grown = jnp.abs(latest[p]) > huge_value
                    latest[p] = jnp.where(grown, latest[p] * tiny_value, latest[p])
                    earlier[p] = jnp.where(grown, earlier[p] * tiny_value, earlier[p])
                    exponent[p] = jnp.where(grown, exponent[p] + 1.0, exponent[p])
                    scale.append(jnp.exp(base[p] + exponent[p] * log_step))
            d = degree.astype(f32)
            width = d * d - square
            inverse = lax.rsqrt(jnp.maximum(width, 1.0))
            gain_a = rise_ref[degree] * inverse
            both = gain_a * gain_b
            start_here = order == degree
            for p in range(wide):
                fresh = (gain_a * cosine[p]) * latest[p] - both * earlier[p]
                fresh = jnp.where(start_here, 1.0, fresh)
                earlier[p] = latest[p]
                latest[p] = fresh
                keep[p, step * m_pad : (step + 1) * m_pad, :] = fresh * scale[p]
            gain_b = fall_ref[degree] * (jnp.maximum(width, 0.0) * inverse)
        for m in range(m_count):
            rows = jnp.concatenate(
                [keep[part, pl.ds(m, 16, stride=m_pad), :] for part in range(wide)], axis=1
            )
            table_ref[m, pl.ds(pl.multiple_of(number * 16, 16), 16), :] = rows.astype(bf16)
        copy_out(number).start()
        return tuple(latest), tuple(earlier), tuple(exponent), gain_b

    zero = jnp.zeros((m_pad, 128), f32)
    zeros = (zero,) * wide
    lax.fori_loop(0, degrees // 16, block, (zeros, zeros, zeros, zero))

    def finish(number, carry):
        copy_out(number).wait()
        return carry

    lax.fori_loop(0, degrees // 16, finish, 0)


def legendre_inputs(degrees, lat_count, row_count):
    nlat = lat_count * row_count
    place = np.arange(nlat)
    t = (place % lat_count) * row_count + place // lat_count
    theta = math.pi * (t + 0.5) / nlat
    counter = np.arange(1, degrees, dtype=np.float64)
    running = np.concatenate([[0.0], np.cumsum(np.log((2 * counter - 1) / (2 * counter)))])
    m = np.arange(degrees)
    norm = 0.5 * np.log((2 * m + 1) / (4 * math.pi)) + 0.5 * running
    rise = np.sqrt(np.maximum(4.0 * m * m - 1.0, 1.0)).astype(np.float32)
    fall = (1.0 / np.sqrt(np.maximum(4.0 * m * m - 1.0, 1.0))).astype(np.float32)
    return (
        jnp.asarray(rise),
        jnp.asarray(fall),
        jnp.asarray(norm.astype(np.float32)),
        jnp.asarray(np.cos(theta)[None].astype(np.float32)),
        jnp.asarray(np.log(np.sin(theta))[None].astype(np.float32)),
    )


def lon_kernel(near_cos_ref, near_sin_ref, far_ref, tab_ref):
    blocks = tab_ref.shape[1] // 128
    for b in range(blocks):
        tab_ref[:, b * 128 : (b + 1) * 128] = (
            near_cos_ref[...] * far_ref[:, b : b + 1]
            - near_sin_ref[...] * far_ref[:, blocks + b : blocks + b + 1]
        ).astype(bf16)


def lon_table(degrees, nlon, owners):
    per = degrees // owners
    row = np.arange(2 * degrees)
    m_np = row // (2 * per) * per + row % per
    m = jnp.asarray(m_np.astype(np.int32))
    shift = jnp.asarray(((row // per % 2) * (nlon // 4)).astype(np.int32))
    low = jnp.arange(128, dtype=jnp.int32)
    angle = (m[:, None] * low[None, :] + shift[:, None]) % nlon
    phase = 2.0 * math.pi / nlon * angle.astype(f32)
    far = 2.0 * math.pi * ((m_np[:, None] * np.arange(nlon // 128)[None] * 128) % nlon) / nlon
    far = np.concatenate([np.cos(far), np.sin(far)], axis=1).astype(np.float32)
    return pl.pallas_call(
        lon_kernel,
        out_shape=jax.ShapeDtypeStruct((2 * degrees, nlon), bf16),
        in_specs=vmem(3),
        out_specs=vmem(1)[0],
        compiler_params=params(),
        cost_estimate=cost(1e8, 3e6),
        name="lon_table",
    )(jnp.cos(phase), jnp.sin(phase), jnp.asarray(far))


def pack_rows(z, k_count):
    third = k_count // 3
    rest = [z[j * third : (j + 1) * third, 256:288] for j in range(3)]
    rest.append(jnp.zeros((third, 32), f32))
    return jnp.concatenate([z[:, 0:128], z[:, 128:256], jnp.concatenate(rest, axis=1)], axis=0)


def analysis_kernel(k_count, cotangent_pass, *refs):
    circ_ref, tab_ref = refs[:2]
    out_ref, keep = refs[-2:]
    sectors = circ_ref.shape[0]
    lines = keep.shape[1]
    owners = out_ref.shape[0]
    height = 2 * k_count + k_count // 3
    if len(circ_ref.shape) == 3:
        parts = [circ_ref[s, 0:lines, :] for s in range(sectors)]
    else:
        parts = [circ_ref[s].astype(f32).reshape(lines, -1).astype(bf16) for s in range(sectors)]
    circ = jnp.concatenate(parts, axis=1)
    z = dot(tab_ref[...], circ, NT)
    if cotangent_pass:
        row = lax.broadcasted_iota(jnp.int32, z.shape, 0)
        z = z * jnp.where((row == 0) | (row == k_count // 2), 1.0, 2.0)
    else:
        z = z * refs[2][...]
    keep[...] = z
    for e in range(owners):
        piece = keep[e * k_count : (e + 1) * k_count, :]
        out_ref[e, 0:height, :] = pack_rows(piece, k_count).astype(bf16)
        if not cotangent_pass:
            out_ref[e, height:, :] = refs[3][e]


def analysis(circ, lines, tab, owners, *field_pass):
    k_count = tab.shape[0] // owners
    height = (2 * k_count + k_count // 3) * (2 if field_pass else 1)
    return pl.pallas_call(
        functools.partial(analysis_kernel, k_count, not field_pass),
        out_shape=jax.ShapeDtypeStruct((owners, height, 128), bf16),
        in_specs=vmem(2 + len(field_pass)),
        out_specs=vmem(1)[0],
        scratch_shapes=[pltpu.VMEM((tab.shape[0], lines), f32)],
        compiler_params=params(),
        cost_estimate=cost(2 * tab.shape[0] * tab.shape[1] * lines, 3e6),
        name="analysis",
    )(circ, tab, *field_pass)


def filter_body(
    m_count, chans, cotangent_pass, idx_ref, lon_ref, recv_ref, weight_ref, post_ref, out_ref,
    took, give, gain, table_ref, flip_ref, ready
):
    places, height, _ = out_ref.shape
    k_count = 2 * m_count
    third = k_count // 3
    nlat = table_ref.shape[1]
    rows = nlat // places
    lane = lax.broadcasted_iota(jnp.int32, (places, 128), 1)

    def load(d, carry):
        at = pl.ds(pl.multiple_of(d * height, 8), height)
        took[at, :] = recv_ref[d, 0:height, :].astype(f32)
        return carry

    lax.fori_loop(0, places, load, 0, unroll=4)
    give[2 * k_count * places :, :] = jnp.zeros((third * places, 128), f32)
    weight = weight_ref[...]
    room = 256 - weight.shape[1]
    weight = jnp.concatenate([weight, jnp.zeros((weight.shape[0], room), f32)], axis=1)
    weight = pltpu.roll(weight, lax.rem(256 - lon_ref[0] * chans, 256), 1)[:, 0:128]
    place = lax.broadcasted_iota(jnp.int32, weight.shape, 1)
    weight = jnp.where(place < chans, weight, 0.0)
    gain[...] = weight + pltpu.roll(weight, chans, 1)

    def one(mm):
        blocks = []
        for r in range(2):
            k = r * m_count + mm
            b0 = took[pl.ds(k, places, stride=height), :]
            b1 = took[pl.ds(k_count + k, places, stride=height), :]
            b2 = took[pl.ds(2 * k_count + k % third, places, stride=height), :]
            b2 = pltpu.roll(b2, (128 - 32 * (k // third)) % 128, 1)
            blocks.append((b0, b1, b2))
        columns = []
        for i in range(rows):
            start = i * chans
            first, last = start // 128, (start + chans - 1) // 128
            total = None
            for q, b in enumerate(blocks):
                if first == last:
                    source = b[first]
                else:
                    source = jnp.where(lane < 64, b[last], b[first])
                shift = (q * chans - start) % 128
                source = pltpu.roll(source, shift, 1) if shift else source
                total = source if total is None else jnp.where(lane < chans, total, source)
            columns.append(total)
        x = jnp.concatenate(columns, axis=0).astype(bf16)
        coeffs = dot(table_ref[mm], x)
        filtered = (coeffs * gain[...]).astype(bf16)
        y = dot(flip_ref[mm], filtered)
        if cotangent_pass:
            y = y * post_ref[...]
        else:
            y = y * jnp.where(idx_ref[0] * m_count + mm == 0, 1.0, 2.0).astype(f32)
        for r in range(2):
            k = r * m_count + mm
            outs = [jnp.zeros((places, 128), f32) for _ in range(3)]
            for i in range(rows):
                start = i * chans
                first, last = start // 128, (start + chans - 1) // 128
                shift = (start - r * chans) % 128
                piece = y[i * places : (i + 1) * places, :]
                piece = pltpu.roll(piece, shift, 1) if shift else piece
                for part in range(first, last + 1):
                    lo, hi = start - part * 128, start + chans - part * 128
                    outs[part] = jnp.where((lane >= lo) & (lane < hi), piece, outs[part])
            give[pl.ds(k * places, places), :] = outs[0]
            give[pl.ds((k_count + k) * places, places), :] = outs[1]
            at = pl.ds((2 * k_count + k % third) * places, places)
            give[at, :] = give[at, :] + pltpu.roll(outs[2], 32 * (k // third), 1)

    def group(number, carry):
        for m in range(3):
            ready(number * 3 + m)
        for m in range(3):
            one(number * 3 + m)
        return carry

    lax.fori_loop(0, m_count // 3, group, 0)

    def store(d, carry):
        out_ref[d] = give[pl.ds(d, height, stride=places), :].astype(bf16)
        return carry

    lax.fori_loop(0, places, store, 0, unroll=4)


def legendre_table(where, legendre, m_count, degrees, nlat):
    smem = pl.BlockSpec(memory_space=pltpu.SMEM)
    return pl.pallas_call(
        functools.partial(legendre_kernel, m_count),
        out_shape=jax.ShapeDtypeStruct((m_count, degrees, nlat), bf16),
        in_specs=[smem] * 4 + vmem(2),
        out_specs=hbm(1)[0],
        scratch_shapes=[
            pltpu.VMEM((nlat // 128, 16 * 16, 128), f32),
            pltpu.VMEM((m_count, degrees, nlat), bf16),
            pltpu.SemaphoreType.DMA((degrees // 16,)),
        ],
        compiler_params=params(60),
        cost_estimate=cost(2e9, 4e6),
        name="legendre_table",
    )(where, *legendre)


def flip_kernel(table_in, flip_out, table, flip, sems):
    orders = table.shape[0]
    for m in range(orders):
        pltpu.make_async_copy(table_in.at[m], table.at[m], sems.at[0, m]).start()

    def turn(m, carry):
        pltpu.make_async_copy(table_in.at[m], table.at[m], sems.at[0, m]).wait()
        flip[m] = jnp.transpose(table[m])
        pltpu.make_async_copy(flip.at[m], flip_out.at[m], sems.at[1, m]).start()
        return carry

    lax.fori_loop(0, orders, turn, 0)
    for m in range(orders):
        pltpu.make_async_copy(flip.at[m], flip_out.at[m], sems.at[1, m]).wait()


def flipped_table(table):
    m_count, degrees, nlat = table.shape
    return pl.pallas_call(
        flip_kernel,
        out_shape=jax.ShapeDtypeStruct((m_count, nlat, degrees), bf16),
        in_specs=hbm(1),
        out_specs=hbm(1)[0],
        scratch_shapes=table_scratch(m_count, degrees, nlat),
        compiler_params=params(60),
        cost_estimate=cost(1e8, 7e6),
        name="flip_table",
    )(table)


def filter_kernel(
    m_count, chans, cotangent_pass, idx_ref, lon_ref, recv_ref, weight_ref, post_ref, table_in,
    flip_in, out_ref, took, give, gain, table, flip, sems
):
    def begin(m, carry):
        pltpu.make_async_copy(table_in.at[m], table.at[m], sems.at[0, m]).start()
        pltpu.make_async_copy(flip_in.at[m], flip.at[m], sems.at[1, m]).start()
        return carry

    lax.fori_loop(0, m_count, begin, 0)

    def ready(m):
        pltpu.make_async_copy(table_in.at[m], table.at[m], sems.at[0, m]).wait()
        pltpu.make_async_copy(flip_in.at[m], flip.at[m], sems.at[1, m]).wait()

    filter_body(
        m_count, chans, cotangent_pass, idx_ref, lon_ref, recv_ref, weight_ref, post_ref, out_ref,
        took, give, gain, table, flip, ready,
    )


def filter_scratch(places, height, degrees):
    return [
        pltpu.VMEM((places * height, 128), f32),
        pltpu.VMEM((places * height, 128), f32),
        pltpu.VMEM((degrees, 128), f32),
    ]


def table_scratch(m_count, degrees, nlat):
    return [
        pltpu.VMEM((m_count, degrees, nlat), bf16),
        pltpu.VMEM((m_count, nlat, degrees), bf16),
        pltpu.SemaphoreType.DMA((2, m_count)),
    ]


def filter_step(where, lon, recv, weight, post, table, flip, chans, cotangent_pass):
    places = recv.shape[0]
    m_count, degrees, nlat = table.shape
    height = 4 * m_count + 2 * m_count // 3
    return pl.pallas_call(
        functools.partial(filter_kernel, m_count, chans, cotangent_pass),
        out_shape=jax.ShapeDtypeStruct((places, height, 128), bf16),
        in_specs=[pl.BlockSpec(memory_space=pltpu.SMEM)] * 2 + vmem(3) + hbm(2),
        out_specs=vmem(1)[0],
        scratch_shapes=[
            *filter_scratch(places, height, degrees),
            *table_scratch(m_count, degrees, nlat),
        ],
        compiler_params=params(60),
        cost_estimate=cost(8e9, 9e6),
        name="filter_step",
    )(where, lon, recv, weight, post, table, flip)


def synthesis_kernel(which, recv_ref, tab_ref, out_ref):
    owners = recv_ref.shape[0]
    k_count = tab_ref.shape[0] // owners
    height = 2 * k_count + k_count // 3
    sectors, rows, chans, cols = out_ref.shape
    left, middle, right = [], [], []
    for e in range(owners):
        v = recv_ref[e, which * height : (which + 1) * height, :].astype(f32)
        left.append(v[0:k_count])
        middle.append(v[k_count : 2 * k_count])
        rest = v[2 * k_count :]
        for j in range(3):
            right.append(pltpu.roll(rest, (128 - 32 * j) % 128, 1) if j else rest)
    flat = [jnp.transpose(jnp.concatenate(part, axis=0)) for part in (left, middle, right)]
    s = jnp.concatenate([flat[0], flat[1], flat[2][0:32]], axis=0).astype(bf16)
    circ = dot(s, tab_ref[...])
    for sector in range(sectors):
        piece = circ[:, sector * cols : (sector + 1) * cols]
        out_ref[sector] = piece.reshape(rows, chans, cols).astype(bf16)


def synthesis(recv, tab, which, shape):
    return pl.pallas_call(
        functools.partial(synthesis_kernel, which),
        out_shape=jax.ShapeDtypeStruct(shape, bf16),
        in_specs=vmem(2),
        out_specs=vmem(1)[0],
        compiler_params=params(),
        cost_estimate=cost(2 * tab.shape[0] * tab.shape[1] * shape[1] * shape[2], 5e6),
        name="synthesis",
    )(recv, tab)


def chunk_blocks(count, edge):
    inner = list(range(edge, count - edge))
    return (
        [list(range(edge))]
        + [inner[k : k + 4] for k in range(0, len(inner), 4)]
        + [list(range(count - edge, count))]
    )


def edge_blocks(flat, edge):
    row = lax.broadcasted_iota(jnp.int32, (16, 128), 0)
    lane = lax.broadcasted_iota(jnp.int32, (16, 128), 1)
    first = []
    last = []
    for chunks in chunk_blocks(flat.shape[0] // 128, edge):
        total = jnp.zeros((16, 128), f32)
        for v, chunk in enumerate(chunks):
            head = (row == 2 * v + lane) & (lane < 2)
            tail = (row - 8 - 2 * v == lane - 126) & (lane >= 126)
            select = jnp.where(head | tail, 1.0, 0.0).astype(bf16)
            total = total + dot(select, flat[chunk * 128 : (chunk + 1) * 128], NT)
        first.append(total[0:8])
        last.append(total[8:16])
    return jnp.concatenate(first, axis=0), jnp.concatenate(last, axis=0)


def start_kernel(edge, idx_ref, cot_ref, field_ref, out_ref):
    sectors, height, cols = out_ref.shape
    rows, channels, _ = cot_ref.shape
    chans = channels // sectors
    body = rows * chans
    field = field_ref[...].reshape(rows * channels, cols)
    first, last = edge_blocks(field, edge)
    for b in range(sectors):
        parts = [cot_ref[i, b * chans : (b + 1) * chans, :].astype(f32) for i in range(rows)]
        right = lax.rem(idx_ref[0] + 1, sectors) == b
        parts.append(jnp.where(right, last, first))
        room = height - body - first.shape[0]
        parts.append(jnp.zeros((room, cols), f32))
        out_ref[b] = jnp.concatenate(parts, axis=0).astype(bf16)


def start_step(lon_index, cot, field, sectors, edge):
    rows, channels, cols = cot.shape
    body = rows * channels // sectors
    blocks = len(chunk_blocks(rows * channels // 128, edge))
    height = -(-(body + 8 * blocks) // 16) * 16
    return pl.pallas_call(
        functools.partial(start_kernel, edge),
        out_shape=jax.ShapeDtypeStruct((sectors, height, cols), bf16),
        in_specs=[pl.BlockSpec(memory_space=pltpu.SMEM)] + vmem(2),
        out_specs=vmem(1)[0],
        compiler_params=params(60),
        cost_estimate=cost(1e8, 2e6),
        name="start",
    )(lon_index[None], cot, field)


def weights_kernel(rim, nlat, adjoint, idx_ref, stencil_ref, mix_ref, band, blend):
    groups, width = mix_ref.shape[0], mix_ref.shape[2]
    taps = mix_ref.shape[1] // width
    k_pad = 16
    ext = stencil_ref.shape[0] // k_pad
    rows = ext - 2 * rim
    span = 2 * rim + 1

    tap = lax.broadcasted_iota(jnp.int32, (span * span, 128), 0)
    slot = lax.broadcasted_iota(jnp.int32, (span * span, 128), 1)
    source = idx_ref[0] * rows - rim + slot % ext
    inside = (source >= 0) & (source < nlat) & (slot < span * ext)
    for i in range(rows):
        total = jnp.zeros((k_pad, 128), f32)
        for line in range(i, i + span) if adjoint else (i + rim,):
            if adjoint:
                hit = (span - 1 - tap // span == slot // ext) & (slot % ext == line)
                hit = hit & (tap % span == i - line + span - 1)
            else:
                hit = (tap // span == slot // ext) & (slot % ext == i + tap % span)
            place = jnp.where(inside & hit, 1.0, 0.0).astype(bf16)
            total = total + dot(stencil_ref[line * k_pad : (line + 1) * k_pad, :], place)
        band[i * k_pad : (i + 1) * k_pad, :] = total.astype(bf16)

    depth = width * k_pad
    pair_row = lax.broadcasted_iota(jnp.int32, (taps * width, depth), 0)
    pair_lane = lax.broadcasted_iota(jnp.int32, (taps * width, depth), 1)
    place = jnp.where(
        pair_lane == (pair_row % width) * k_pad + pair_row // width, 1.0, 0.0
    ).astype(bf16)
    for g in range(groups):
        blend[g] = dot(mix_ref[g], place, TN).astype(bf16)


def conv_weights(where, stencil, mix, rim, nlat, adjoint):
    groups, _, width = mix.shape
    return pl.pallas_call(
        functools.partial(weights_kernel, rim, nlat, adjoint),
        out_shape=(
            jax.ShapeDtypeStruct((stencil.shape[0] - 32 * rim, 128), bf16),
            jax.ShapeDtypeStruct((groups, width, width * 16), bf16),
        ),
        in_specs=[pl.BlockSpec(memory_space=pltpu.SMEM)] + vmem(2),
        out_specs=tuple(vmem(2)),
        compiler_params=params(),
        cost_estimate=cost(4e8, 1e6),
        name="conv_weights",
    )(where, stencil, mix)


def conv_body(
    x_ref, low_ref, high_ref, left_ref, right_ref, band_ref, blend_ref, xs, hs, resp, emit
):
    rows, channels, cols = x_ref.shape
    groups, width, _ = blend_ref.shape
    ext = hs.shape[0] // channels
    rim = (ext - rows) // 2
    span = 2 * rim + 1
    edge = rim * channels // 128
    k_pad = 16
    xs[0 : rim * channels, :] = low_ref[0 : rim * channels].astype(f32)
    xs[rim * channels : (rim + rows) * channels, :] = (
        x_ref[...].astype(f32).reshape(rows * channels, cols)
    )
    xs[(rim + rows) * channels :, :] = high_ref[0 : rim * channels].astype(f32)

    row = lax.broadcasted_iota(jnp.int32, (16, cols), 0)
    lane = lax.broadcasted_iota(jnp.int32, (16, cols), 1)

    def spread(left, right, chunks, base):
        turned = jnp.transpose(jnp.concatenate([left.astype(f32), right.astype(f32)], axis=0))
        turned = turned.astype(bf16)
        for v, chunk in enumerate(chunks):
            ahead = (row - 2 * v == lane - (cols - 2)) & (lane >= cols - 2)
            behind = (row - 8 - 2 * v == lane) & (lane < 2)
            put = jnp.where(ahead | behind, 1.0, 0.0).astype(bf16)
            at = (base + chunk) * 128
            hs[at : at + 128, :] = dot(turned, put)

    lists = chunk_blocks(rows * channels // 128, edge)
    tail = rim * channels
    spread(low_ref[tail : tail + 8], low_ref[tail + 8 : tail + 16], range(edge), 0)
    spread(high_ref[tail : tail + 8], high_ref[tail + 8 : tail + 16], range(edge),
           edge + rows * channels // 128)
    for u, chunks in enumerate(lists):
        at = slice(8 * u, 8 * u + 8)
        spread(left_ref[at], right_ref[at], chunks, edge)

    stencil = band_ref[:, 0 : span * ext]

    def column(c):
        x = xs[pl.ds(c, ext, stride=channels), :]
        h = hs[pl.ds(c, ext, stride=channels), :]
        pieces = []
        for s in range(-rim, rim + 1):
            if s == 0:
                pieces.append(x)
                continue
            beyond = lane < s if s > 0 else lane >= cols + s
            pieces.append(pltpu.roll(jnp.where(beyond, h, x), (-s) % cols, 1))
        return jnp.concatenate([p.astype(bf16) for p in pieces], axis=0)

    for g in range(groups):

        def pair(number, carry):
            c = g * width + 2 * number
            both = jnp.concatenate([column(c), column(c + 1)], axis=1)
            r = dot(stencil, both).astype(bf16)
            at = pl.multiple_of(number * 2 * k_pad, k_pad)
            resp[:, pl.ds(at, k_pad), :] = r[:, 0:cols].reshape(rows, k_pad, cols)
            resp[:, pl.ds(at + k_pad, k_pad), :] = r[:, cols:].reshape(rows, k_pad, cols)
            return carry

        lax.fori_loop(0, width // 2, pair, 0, unroll=8)
        for i in range(0, rows, 2):
            operand = jnp.concatenate([resp[i], resp[i + 1]], axis=1)
            out = dot(blend_ref[g], operand)
            emit(g, i, out[:, 0:cols])
            emit(g, i + 1, out[:, cols:])


def forward_kernel(rim, nlat, *refs):
    where_ref, stencil_ref, mix_ref = refs[:3]
    act_ref, slope_ref, xs, hs, resp, band, blend = refs[8:]
    weights_kernel(rim, nlat, False, where_ref, stencil_ref, mix_ref, band, blend)
    width = blend.shape[1]
    chans = act_ref.shape[2]
    root = math.sqrt(2.0 / math.pi)

    def emit(g, i, v):
        square = v * v
        t = jnp.tanh(root * v * (1.0 + 0.044715 * square))
        half = 0.5 * (1.0 + t)
        act = v * half
        slope_ref[i, g * width : (g + 1) * width, :] = half + 0.5 * v * (1.0 - t * t) * (
            root + (root * 3.0 * 0.044715) * square
        )
        for j in range(width // chans):
            act_ref[g * (width // chans) + j, i] = act[j * chans : (j + 1) * chans, :].astype(bf16)

    conv_body(*refs[3:8], band, blend, xs, hs, resp, emit)


def adjoint_kernel(*refs):
    cot_ref, grad_ref = refs[7:9]
    width = refs[6].shape[1]

    def emit(g, i, v):
        at = slice(g * width, (g + 1) * width)
        grad_ref[i, at, :] = (cot_ref[i, at, :].astype(f32) + v).astype(bf16)

    conv_body(*refs[:7], *refs[9:12], emit)


def conv_scratch(rim, x, width):
    rows, channels, cols = x.shape
    flat = (rows + 2 * rim) * channels
    return [
        pltpu.VMEM((flat, cols), f32),
        pltpu.VMEM((flat, cols), f32),
        pltpu.VMEM((rows, width * 16, cols), bf16),
    ]


def conv_forward(where, stencil, mix, rim, nlat, x, halo, shape):
    groups, _, width = mix.shape
    return pl.pallas_call(
        functools.partial(forward_kernel, rim, nlat),
        out_shape=(jax.ShapeDtypeStruct(shape, bf16), jax.ShapeDtypeStruct(x.shape, f32)),
        in_specs=[pl.BlockSpec(memory_space=pltpu.SMEM)] + vmem(7),
        out_specs=tuple(vmem(2)),
        scratch_shapes=[
            *conv_scratch(rim, x, width),
            pltpu.VMEM((x.shape[0] * 16, 128), bf16),
            pltpu.VMEM((groups, width, width * 16), bf16),
        ],
        compiler_params=params(),
        cost_estimate=cost(1.2e10, 4e6),
        name="conv_forward",
    )(where, stencil, mix, x, *halo)


def conv_adjoint(weights, rim, x, halo, cot):
    return pl.pallas_call(
        adjoint_kernel,
        out_shape=jax.ShapeDtypeStruct(x.shape, bf16),
        in_specs=vmem(8),
        out_specs=vmem(1)[0],
        scratch_shapes=conv_scratch(rim, x, weights[1].shape[1]),
        compiler_params=params(),
        cost_estimate=cost(1.2e10, 4e6),
        name="conv_adjoint",
    )(x, *halo, *weights, cot)


def shifted(axis, step):
    count = lax.axis_size(axis)
    return [(a, (a + step) % count) for a in range(count)]


def lat_rims(x, left, right, rim):
    rows, channels, cols = x.shape
    low = jnp.concatenate([x[-rim:].reshape(rim * channels, cols), left[-8:], right[-8:]], axis=0)
    high = jnp.concatenate([x[:rim].reshape(rim * channels, cols), left[:8], right[:8]], axis=0)
    low = lax.ppermute(low, "lat", shifted("lat", 1))
    high = lax.ppermute(high, "lat", shifted("lat", -1))
    return low, high, left, right


def slope_kernel(edge, act_ref, slope_ref, out_ref, left_ref, right_ref):
    blocks, rows, chans, cols = act_ref.shape
    channels = blocks * chans

    def one(i, carry):
        parts = [act_ref[b, i].astype(f32) for b in range(blocks)]
        out_ref[i] = (slope_ref[i] * jnp.concatenate(parts, axis=0)).astype(bf16)
        return carry

    lax.fori_loop(0, rows, one, 0)
    first, last = edge_blocks(out_ref[...].reshape(rows * channels, cols), edge)
    left_ref[...] = first.astype(bf16)
    right_ref[...] = last.astype(bf16)


def slope_step(cot_act, slope, edge):
    rows, channels, cols = slope.shape
    blocks = len(chunk_blocks(rows * channels // 128, edge))
    shape = jax.ShapeDtypeStruct((8 * blocks, cols), bf16)
    return pl.pallas_call(
        functools.partial(slope_kernel, edge),
        out_shape=(jax.ShapeDtypeStruct(slope.shape, bf16), shape, shape),
        in_specs=vmem(2),
        out_specs=tuple(vmem(3)),
        compiler_params=params(),
        cost_estimate=cost(1e8, 3e6),
        name="slope_step",
    )(cot_act, slope)


def stencil_rows(weights):
    rows, span, _, k_count = weights.shape
    w = jnp.transpose(weights, (0, 3, 2, 1)).reshape(rows, k_count, span * span)
    w = jnp.pad(w, ((0, 0), (0, 16 - k_count), (0, 0)))
    return w.reshape(rows * 16, span * span).astype(bf16)


def local(input_field, basis_values, support_reach, mix_weight, filter_weight, cotangent):
    _, rows, channels, cols = input_field.shape
    rim = basis_values.shape[1] // 2
    degrees = filter_weight.shape[0]
    groups, k_count, width, _ = mix_weight.shape
    lat_count = lax.axis_size("lat")
    lon_count = lax.axis_size("lon")
    nlat = rows * lat_count
    nlon = cols * lon_count
    lat_index = lax.axis_index("lat")
    lon_index = lax.axis_index("lon")
    m_count = degrees // lat_count
    chans = channels // lon_count
    row_start = lat_index * rows
    field = input_field[0]
    cot = cotangent[0]

    edge = rim * channels // 128
    body = rows * chans

    sent = start_step(lon_index, cot, field, lon_count, edge)
    circ_c = lax.all_to_all(sent, "lon", 0, 0, tiled=True)

    blocks = 8 * len(chunk_blocks(rows * channels // 128, edge))
    strips = circ_c[:, body : body + blocks]
    left = lax.dynamic_index_in_dim(strips, (lon_index + lon_count - 1) % lon_count, 0, False)
    right = lax.dynamic_index_in_dim(strips, (lon_index + 1) % lon_count, 0, False)
    offsets = jnp.abs(jnp.arange(2 * rim + 1, dtype=jnp.int32) - rim)
    pad = ((rim, rim), (0, 0), (0, 0), (0, 0))
    basis_ext = lax.dynamic_slice_in_dim(jnp.pad(basis_values, pad), row_start, rows + 2 * rim, 0)
    reach_ext = lax.dynamic_slice_in_dim(
        jnp.pad(support_reach, pad[:2]), row_start, rows + 2 * rim, 0
    )
    inside = offsets[None, None, :] <= reach_ext[:, :, None]
    weights_ext = jnp.where(inside[..., None], basis_ext, 0.0)
    stencil = stencil_rows(weights_ext)
    mix = mix_weight.reshape(groups, k_count * width, width)
    mix_adj = jnp.transpose(mix_weight, (0, 1, 3, 2)).reshape(groups, k_count * width, width)
    where = lat_index[None]
    tab = lon_table(degrees, nlon, lat_count)
    legendre = legendre_inputs(degrees, lat_count, rows)
    theta = math.pi * (np.arange(nlat) + 0.5) / nlat
    quad = 2.0 * math.pi * math.pi / nlat * np.sin(theta) / nlon
    quad_rows = np.repeat(quad.reshape(lat_count, rows), chans, axis=1).astype(np.float32)
    post = np.broadcast_to(quad.reshape(lat_count, rows).T.reshape(nlat, 1), (nlat, 128))
    post = jnp.asarray(post.astype(np.float32))
    here = lat_index[None]
    shape = (lon_count, rows, chans, cols)

    table = legendre_table(here, legendre, m_count, degrees, nlat)
    circ_c, table = lax.optimization_barrier((circ_c, table))
    send_1 = analysis(circ_c, body, tab, lat_count)
    halo = lat_rims(field, left, right, rim)
    send_1, halo = lax.optimization_barrier((send_1, halo))
    recv_1 = lax.all_to_all(send_1, "lat", 0, 0, tiled=True)
    act, slope = conv_forward(where, stencil, mix, rim, nlat, field, halo, shape)
    act, table, filter_weight, later = lax.optimization_barrier(
        (act, table, filter_weight, lat_index)
    )
    quad_lanes = lax.dynamic_slice_in_dim(jnp.asarray(quad_rows), later, 1, 0)
    flip = flipped_table(table)
    recv_1, act, table, flip = lax.optimization_barrier((recv_1, act, table, flip))
    circ_f = lax.all_to_all(act, "lon", 0, 0, tiled=True)
    filtered_c = filter_step(here, lon_index[None], recv_1, filter_weight, post, table, flip, chans, True)
    send_2 = analysis(circ_f, body, tab, lat_count, quad_lanes, filtered_c)
    recv_2 = lax.all_to_all(send_2, "lat", 0, 0, tiled=True)
    stencil, send_2 = lax.optimization_barrier((stencil, send_2))
    weights_adj = conv_weights(where, stencil, mix_adj, rim, nlat, True)
    recv_2, weights_adj = lax.optimization_barrier((recv_2, weights_adj))
    cot_act = lax.all_to_all(synthesis(recv_2, tab, 1, shape), "lon", 0, 0, tiled=True)
    filtered_f = filter_step(here, lon_index[None], recv_2, filter_weight, post, table, flip, chans, False)
    recv_3 = lax.all_to_all(filtered_f, "lat", 0, 0, tiled=True)
    branch = lax.all_to_all(synthesis(recv_3, tab, 0, shape), "lon", 0, 0, tiled=True)

    cot_conv, first_c, last_c = slope_step(cot_act, slope, edge)
    left_c = lax.ppermute(last_c, "lon", shifted("lon", 1))
    right_c = lax.ppermute(first_c, "lon", shifted("lon", -1))
    halo_c = lat_rims(cot_conv, left_c, right_c, rim)
    grad_field = conv_adjoint(weights_adj, rim, cot_conv, halo_c, cot)
    branch = jnp.transpose(branch, (1, 0, 2, 3)).reshape(rows, channels, cols)
    block_out = (field.astype(f32) + branch.astype(f32)).astype(bf16)
    return block_out[None], grad_field[None]


def solution(mesh):
    placed = (P(None, "lat", None, "lon"), P(), P(), P(), P(), P(None, "lat", None, "lon"))
    return jax.shard_map(
        local,
        mesh=mesh,
        in_specs=placed,
        out_specs=(P(None, "lat", None, "lon"), P(None, "lat", None, "lon")),
        check_vma=False,
    )
```

```python
import functools
import math

import jax
import jax.numpy as jnp
import numpy as np
from jax import lax
from jax.experimental import pallas as pl
from jax.experimental.pallas import tpu as pltpu
from jax.sharding import PartitionSpec as P

huge_value = 2.0**60
tiny_value = 2.0 ** (-60)
log_step = 41.58883083359672

f32 = jnp.float32
bf16 = jnp.bfloat16

NT = (((1,), (1,)), ((), ()))
NN = (((1,), (0,)), ((), ()))
TN = (((0,), (0,)), ((), ()))


def dot(a, b, dims=NN):
    return lax.dot_general(a, b, dims, preferred_element_type=f32)


def params(mib=20):
    return pltpu.CompilerParams(vmem_limit_bytes=mib * 1024 * 1024)


def vmem(count):
    return [pl.BlockSpec(memory_space=pltpu.VMEM)] * count


def hbm(count):
    return [pl.BlockSpec(memory_space=pl.ANY)] * count


def cost(flops, nbytes):
    return pl.CostEstimate(flops=int(flops), bytes_accessed=int(nbytes), transcendentals=0)


def legendre_kernel(
    m_count, idx_ref, rise_ref, fall_ref, norm_ref, cos_ref, logsin_ref, table_out,
    keep, table_ref, sems
):
    m_pad, lat = 16, cos_ref.shape[1]
    degrees = table_ref.shape[1]
    wide = lat // 128
    first = idx_ref[0] * m_count
    order = first + lax.broadcasted_iota(jnp.int32, (m_pad, 128), 0)
    order_real = order.astype(f32)
    square = order_real * order_real
    cosine = [
        jnp.broadcast_to(cos_ref[:, p * 128 : (p + 1) * 128], (m_pad, 128)) for p in range(wide)
    ]
    local_row = lax.broadcasted_iota(jnp.int32, (m_pad, 128), 0)
    norm = jnp.zeros((m_pad, 128), f32)
    for m in range(m_count):
        norm = jnp.where(local_row == m, norm_ref[first + m], norm)
    base = [
        norm + order_real * logsin_ref[:, p * 128 : (p + 1) * 128] for p in range(wide)
    ]

    def copy_out(number):
        at = pl.ds(pl.multiple_of(number * 16, 16), 16)
        return pltpu.make_async_copy(table_ref.at[:, at], table_out.at[:, at], sems.at[number])

    def block(number, carry):
        latest, earlier, exponent, gain_b = carry
        latest, earlier, exponent = list(latest), list(earlier), list(exponent)
        for step in range(16):
            degree = number * 16 + step
            if step % 4 == 0:
                scale = []
                for p in range(wide):
                    grown = jnp.abs(latest[p]) > huge_value
                    latest[p] = jnp.where(grown, latest[p] * tiny_value, latest[p])
                    earlier[p] = jnp.where(grown, earlier[p] * tiny_value, earlier[p])
                    exponent[p] = jnp.where(grown, exponent[p] + 1.0, exponent[p])
                    scale.append(jnp.exp(base[p] + exponent[p] * log_step))
            d = degree.astype(f32)
            width = d * d - square
            inverse = lax.rsqrt(jnp.maximum(width, 1.0))
            gain_a = rise_ref[degree] * inverse
            both = gain_a * gain_b
            start_here = order == degree
            for p in range(wide):
                fresh = (gain_a * cosine[p]) * latest[p] - both * earlier[p]
                fresh = jnp.where(start_here, 1.0, fresh)
                earlier[p] = latest[p]
                latest[p] = fresh
                keep[p, step * m_pad : (step + 1) * m_pad, :] = fresh * scale[p]
            gain_b = fall_ref[degree] * (jnp.maximum(width, 0.0) * inverse)
        for m in range(m_count):
            rows = jnp.concatenate(
                [keep[part, pl.ds(m, 16, stride=m_pad), :] for part in range(wide)], axis=1
            )
            table_ref[m, pl.ds(pl.multiple_of(number * 16, 16), 16), :] = rows.astype(bf16)
        copy_out(number).start()
        return tuple(latest), tuple(earlier), tuple(exponent), gain_b

    zero = jnp.zeros((m_pad, 128), f32)
    zeros = (zero,) * wide
    lax.fori_loop(0, degrees // 16, block, (zeros, zeros, zeros, zero))

    def finish(number, carry):
        copy_out(number).wait()
        return carry

    lax.fori_loop(0, degrees // 16, finish, 0)


def legendre_inputs(degrees, lat_count, row_count):
    nlat = lat_count * row_count
    place = np.arange(nlat)
    t = (place % lat_count) * row_count + place // lat_count
    theta = math.pi * (t + 0.5) / nlat
    counter = np.arange(1, degrees, dtype=np.float64)
    running = np.concatenate([[0.0], np.cumsum(np.log((2 * counter - 1) / (2 * counter)))])
    m = np.arange(degrees)
    norm = 0.5 * np.log((2 * m + 1) / (4 * math.pi)) + 0.5 * running
    rise = np.sqrt(np.maximum(4.0 * m * m - 1.0, 1.0)).astype(np.float32)
    fall = (1.0 / np.sqrt(np.maximum(4.0 * m * m - 1.0, 1.0))).astype(np.float32)
    return (
        jnp.asarray(rise),
        jnp.asarray(fall),
        jnp.asarray(norm.astype(np.float32)),
        jnp.asarray(np.cos(theta)[None].astype(np.float32)),
        jnp.asarray(np.log(np.sin(theta))[None].astype(np.float32)),
    )


def lon_kernel(near_cos_ref, near_sin_ref, far_ref, tab_ref):
    blocks = tab_ref.shape[1] // 128
    for b in range(blocks):
        tab_ref[:, b * 128 : (b + 1) * 128] = (
            near_cos_ref[...] * far_ref[:, b : b + 1]
            - near_sin_ref[...] * far_ref[:, blocks + b : blocks + b + 1]
        ).astype(bf16)


def lon_table(degrees, nlon, owners):
    per = degrees // owners
    row = np.arange(2 * degrees)
    m_np = row // (2 * per) * per + row % per
    m = jnp.asarray(m_np.astype(np.int32))
    shift = jnp.asarray(((row // per % 2) * (nlon // 4)).astype(np.int32))
    low = jnp.arange(128, dtype=jnp.int32)
    angle = (m[:, None] * low[None, :] + shift[:, None]) % nlon
    phase = 2.0 * math.pi / nlon * angle.astype(f32)
    far = 2.0 * math.pi * ((m_np[:, None] * np.arange(nlon // 128)[None] * 128) % nlon) / nlon
    far = np.concatenate([np.cos(far), np.sin(far)], axis=1).astype(np.float32)
    return pl.pallas_call(
        lon_kernel,
        out_shape=jax.ShapeDtypeStruct((2 * degrees, nlon), bf16),
        in_specs=vmem(3),
        out_specs=vmem(1)[0],
        compiler_params=params(),
        cost_estimate=cost(1e8, 3e6),
        name="lon_table",
    )(jnp.cos(phase), jnp.sin(phase), jnp.asarray(far))


def pack_rows(z, k_count):
    third = k_count // 3
    rest = [z[j * third : (j + 1) * third, 256:288] for j in range(3)]
    rest.append(jnp.zeros((third, 32), f32))
    return jnp.concatenate([z[:, 0:128], z[:, 128:256], jnp.concatenate(rest, axis=1)], axis=0)


def analysis_kernel(k_count, cotangent_pass, *refs):
    circ_ref, tab_ref = refs[:2]
    out_ref, keep = refs[-2:]
    sectors = circ_ref.shape[0]
    lines = keep.shape[1]
    owners = out_ref.shape[0]
    height = 2 * k_count + k_count // 3
    if len(circ_ref.shape) == 3:
        parts = [circ_ref[s, 0:lines, :] for s in range(sectors)]
    else:
        parts = [circ_ref[s].astype(f32).reshape(lines, -1).astype(bf16) for s in range(sectors)]
    circ = jnp.concatenate(parts, axis=1)
    z = dot(tab_ref[...], circ, NT)
    if cotangent_pass:
        row = lax.broadcasted_iota(jnp.int32, z.shape, 0)
        z = z * jnp.where((row == 0) | (row == k_count // 2), 1.0, 2.0)
    else:
        z = z * refs[2][...]
    keep[...] = z
    for e in range(owners):
        piece = keep[e * k_count : (e + 1) * k_count, :]
        out_ref[e, 0:height, :] = pack_rows(piece, k_count).astype(bf16)
        if not cotangent_pass:
            out_ref[e, height:, :] = refs[3][e]


def analysis(circ, lines, tab, owners, *field_pass):
    k_count = tab.shape[0] // owners
    height = (2 * k_count + k_count // 3) * (2 if field_pass else 1)
    return pl.pallas_call(
        functools.partial(analysis_kernel, k_count, not field_pass),
        out_shape=jax.ShapeDtypeStruct((owners, height, 128), bf16),
        in_specs=vmem(2 + len(field_pass)),
        out_specs=vmem(1)[0],
        scratch_shapes=[pltpu.VMEM((tab.shape[0], lines), f32)],
        compiler_params=params(),
        cost_estimate=cost(2 * tab.shape[0] * tab.shape[1] * lines, 3e6),
        name="analysis",
    )(circ, tab, *field_pass)


def filter_body(
    m_count, chans, cotangent_pass, idx_ref, lon_ref, recv_ref, weight_ref, post_ref, out_ref,
    took, give, gain, table_ref, flip_ref, ready
):
    places, height, _ = out_ref.shape
    k_count = 2 * m_count
    third = k_count // 3
    nlat = table_ref.shape[1]
    rows = nlat // places
    lane = lax.broadcasted_iota(jnp.int32, (places, 128), 1)

    def load(d, carry):
        at = pl.ds(pl.multiple_of(d * height, 8), height)
        took[at, :] = recv_ref[d, 0:height, :].astype(f32)
        return carry

    lax.fori_loop(0, places, load, 0, unroll=4)
    give[2 * k_count * places :, :] = jnp.zeros((third * places, 128), f32)
    at = pl.ds(pl.multiple_of(lon_ref[0] * chans, 8), chans)
    weight = weight_ref[at, :]
    room = jnp.zeros((128 - 2 * chans, weight.shape[1]), f32)
    gain[...] = jnp.transpose(jnp.concatenate([weight, weight, room], axis=0))

    def one(mm):
        blocks = []
        for r in range(2):
            k = r * m_count + mm
            b0 = took[pl.ds(k, places, stride=height), :]
            b1 = took[pl.ds(k_count + k, places, stride=height), :]
            b2 = took[pl.ds(2 * k_count + k % third, places, stride=height), :]
            b2 = pltpu.roll(b2, (128 - 32 * (k // third)) % 128, 1)
            blocks.append((b0, b1, b2))
        columns = []
        for i in range(rows):
            start = i * chans
            first, last = start // 128, (start + chans - 1) // 128
            total = None
            for q, b in enumerate(blocks):
                if first == last:
                    source = b[first]
                else:
                    source = jnp.where(lane < 64, b[last], b[first])
                shift = (q * chans - start) % 128
                source = pltpu.roll(source, shift, 1) if shift else source
                total = source if total is None else jnp.where(lane < chans, total, source)
            columns.append(total)
        x = jnp.concatenate(columns, axis=0).astype(bf16)
        coeffs = dot(table_ref[mm], x)
        filtered = (coeffs * gain[...]).astype(bf16)
        y = dot(flip_ref[mm], filtered)
        if cotangent_pass:
            y = y * post_ref[...]
        else:
            y = y * jnp.where(idx_ref[0] * m_count + mm == 0, 1.0, 2.0).astype(f32)
        for r in range(2):
            k = r * m_count + mm
            outs = [jnp.zeros((places, 128), f32) for _ in range(3)]
            for i in range(rows):
                start = i * chans
                first, last = start // 128, (start + chans - 1) // 128
                shift = (start - r * chans) % 128
                piece = y[i * places : (i + 1) * places, :]
                piece = pltpu.roll(piece, shift, 1) if shift else piece
                for part in range(first, last + 1):
                    lo, hi = start - part * 128, start + chans - part * 128
                    outs[part] = jnp.where((lane >= lo) & (lane < hi), piece, outs[part])
            give[pl.ds(k * places, places), :] = outs[0]
            give[pl.ds((k_count + k) * places, places), :] = outs[1]
            at = pl.ds((2 * k_count + k % third) * places, places)
            give[at, :] = give[at, :] + pltpu.roll(outs[2], 32 * (k // third), 1)

    def group(number, carry):
        for m in range(3):
            ready(number * 3 + m)
        for m in range(3):
            one(number * 3 + m)
        return carry

    lax.fori_loop(0, m_count // 3, group, 0)

    def store(d, carry):
        out_ref[d] = give[pl.ds(d, height, stride=places), :].astype(bf16)
        return carry

    lax.fori_loop(0, places, store, 0, unroll=4)


def legendre_table(where, legendre, m_count, degrees, nlat):
    smem = pl.BlockSpec(memory_space=pltpu.SMEM)
    return pl.pallas_call(
        functools.partial(legendre_kernel, m_count),
        out_shape=jax.ShapeDtypeStruct((m_count, degrees, nlat), bf16),
        in_specs=[smem] * 4 + vmem(2),
        out_specs=hbm(1)[0],
        scratch_shapes=[
            pltpu.VMEM((nlat // 128, 16 * 16, 128), f32),
            pltpu.VMEM((m_count, degrees, nlat), bf16),
            pltpu.SemaphoreType.DMA((degrees // 16,)),
        ],
        compiler_params=params(60),
        cost_estimate=cost(2e9, 4e6),
        name="legendre_table",
    )(where, *legendre)


def flip_kernel(table_in, flip_out, table, flip, sems):
    orders = table.shape[0]
    for m in range(orders):
        pltpu.make_async_copy(table_in.at[m], table.at[m], sems.at[0, m]).start()

    def turn(m, carry):
        pltpu.make_async_copy(table_in.at[m], table.at[m], sems.at[0, m]).wait()
        flip[m] = jnp.transpose(table[m])
        pltpu.make_async_copy(flip.at[m], flip_out.at[m], sems.at[1, m]).start()
        return carry

    lax.fori_loop(0, orders, turn, 0)
    for m in range(orders):
        pltpu.make_async_copy(flip.at[m], flip_out.at[m], sems.at[1, m]).wait()


def flipped_table(table):
    m_count, degrees, nlat = table.shape
    return pl.pallas_call(
        flip_kernel,
        out_shape=jax.ShapeDtypeStruct((m_count, nlat, degrees), bf16),
        in_specs=hbm(1),
        out_specs=hbm(1)[0],
        scratch_shapes=table_scratch(m_count, degrees, nlat),
        compiler_params=params(60),
        cost_estimate=cost(1e8, 7e6),
        name="flip_table",
    )(table)


def filter_kernel(
    m_count, chans, cotangent_pass, idx_ref, lon_ref, recv_ref, weight_ref, post_ref, table_in,
    flip_in, out_ref, took, give, gain, table, flip, sems
):
    def begin(m, carry):
        pltpu.make_async_copy(table_in.at[m], table.at[m], sems.at[0, m]).start()
        pltpu.make_async_copy(flip_in.at[m], flip.at[m], sems.at[1, m]).start()
        return carry

    lax.fori_loop(0, m_count, begin, 0)

    def ready(m):
        pltpu.make_async_copy(table_in.at[m], table.at[m], sems.at[0, m]).wait()
        pltpu.make_async_copy(flip_in.at[m], flip.at[m], sems.at[1, m]).wait()

    filter_body(
        m_count, chans, cotangent_pass, idx_ref, lon_ref, recv_ref, weight_ref, post_ref, out_ref,
        took, give, gain, table, flip, ready,
    )


def filter_scratch(places, height, degrees):
    return [
        pltpu.VMEM((places * height, 128), f32),
        pltpu.VMEM((places * height, 128), f32),
        pltpu.VMEM((degrees, 128), f32),
    ]


def table_scratch(m_count, degrees, nlat):
    return [
        pltpu.VMEM((m_count, degrees, nlat), bf16),
        pltpu.VMEM((m_count, nlat, degrees), bf16),
        pltpu.SemaphoreType.DMA((2, m_count)),
    ]


def filter_step(where, lon, recv, weight, post, table, flip, chans, cotangent_pass):
    places = recv.shape[0]
    m_count, degrees, nlat = table.shape
    height = 4 * m_count + 2 * m_count // 3
    weight = jnp.transpose(weight)
    return pl.pallas_call(
        functools.partial(filter_kernel, m_count, chans, cotangent_pass),
        out_shape=jax.ShapeDtypeStruct((places, height, 128), bf16),
        in_specs=[pl.BlockSpec(memory_space=pltpu.SMEM)] * 2 + vmem(3) + hbm(2),
        out_specs=vmem(1)[0],
        scratch_shapes=[
            *filter_scratch(places, height, degrees),
            *table_scratch(m_count, degrees, nlat),
        ],
        compiler_params=params(60),
        cost_estimate=cost(8e9, 9e6),
        name="filter_step",
    )(where, lon, recv, weight, post, table, flip)


def synthesis_kernel(which, recv_ref, tab_ref, out_ref):
    owners = recv_ref.shape[0]
    k_count = tab_ref.shape[0] // owners
    height = 2 * k_count + k_count // 3
    sectors, rows, chans, cols = out_ref.shape
    left, middle, right = [], [], []
    for e in range(owners):
        v = recv_ref[e, which * height : (which + 1) * height, :].astype(f32)
        left.append(v[0:k_count])
        middle.append(v[k_count : 2 * k_count])
        rest = v[2 * k_count :]
        for j in range(3):
            right.append(pltpu.roll(rest, (128 - 32 * j) % 128, 1) if j else rest)
    flat = [jnp.transpose(jnp.concatenate(part, axis=0)) for part in (left, middle, right)]
    s = jnp.concatenate([flat[0], flat[1], flat[2][0:32]], axis=0).astype(bf16)
    circ = dot(s, tab_ref[...])
    for sector in range(sectors):
        piece = circ[:, sector * cols : (sector + 1) * cols]
        out_ref[sector] = piece.reshape(rows, chans, cols).astype(bf16)


def synthesis(recv, tab, which, shape):
    return pl.pallas_call(
        functools.partial(synthesis_kernel, which),
        out_shape=jax.ShapeDtypeStruct(shape, bf16),
        in_specs=vmem(2),
        out_specs=vmem(1)[0],
        compiler_params=params(),
        cost_estimate=cost(2 * tab.shape[0] * tab.shape[1] * shape[1] * shape[2], 5e6),
        name="synthesis",
    )(recv, tab)


def chunk_blocks(count, edge):
    inner = list(range(edge, count - edge))
    return (
        [list(range(edge))]
        + [inner[k : k + 4] for k in range(0, len(inner), 4)]
        + [list(range(count - edge, count))]
    )


def edge_blocks(flat, edge):
    row = lax.broadcasted_iota(jnp.int32, (16, 128), 0)
    lane = lax.broadcasted_iota(jnp.int32, (16, 128), 1)
    first = []
    last = []
    for chunks in chunk_blocks(flat.shape[0] // 128, edge):
        total = jnp.zeros((16, 128), f32)
        for v, chunk in enumerate(chunks):
            head = (row == 2 * v + lane) & (lane < 2)
            tail = (row - 8 - 2 * v == lane - 126) & (lane >= 126)
            select = jnp.where(head | tail, 1.0, 0.0).astype(bf16)
            total = total + dot(select, flat[chunk * 128 : (chunk + 1) * 128], NT)
        first.append(total[0:8])
        last.append(total[8:16])
    return jnp.concatenate(first, axis=0), jnp.concatenate(last, axis=0)


def start_kernel(edge, idx_ref, cot_ref, field_ref, out_ref):
    sectors, height, cols = out_ref.shape
    rows, channels, _ = cot_ref.shape
    chans = channels // sectors
    body = rows * chans
    field = field_ref[...].reshape(rows * channels, cols)
    first, last = edge_blocks(field, edge)
    for b in range(sectors):
        parts = [cot_ref[i, b * chans : (b + 1) * chans, :].astype(f32) for i in range(rows)]
        right = lax.rem(idx_ref[0] + 1, sectors) == b
        parts.append(jnp.where(right, last, first))
        room = height - body - first.shape[0]
        parts.append(jnp.zeros((room, cols), f32))
        out_ref[b] = jnp.concatenate(parts, axis=0).astype(bf16)


def start_step(lon_index, cot, field, sectors, edge):
    rows, channels, cols = cot.shape
    body = rows * channels // sectors
    blocks = len(chunk_blocks(rows * channels // 128, edge))
    height = -(-(body + 8 * blocks) // 16) * 16
    return pl.pallas_call(
        functools.partial(start_kernel, edge),
        out_shape=jax.ShapeDtypeStruct((sectors, height, cols), bf16),
        in_specs=[pl.BlockSpec(memory_space=pltpu.SMEM)] + vmem(2),
        out_specs=vmem(1)[0],
        compiler_params=params(60),
        cost_estimate=cost(1e8, 2e6),
        name="start",
    )(lon_index[None], cot, field)


def weights_kernel(rim, nlat, adjoint, idx_ref, stencil_ref, mix_ref, band, blend):
    groups, width = mix_ref.shape[0], mix_ref.shape[2]
    taps = mix_ref.shape[1] // width
    k_pad = 16
    ext = stencil_ref.shape[0] // k_pad
    rows = ext - 2 * rim
    span = 2 * rim + 1

    tap = lax.broadcasted_iota(jnp.int32, (span * span, 128), 0)
    slot = lax.broadcasted_iota(jnp.int32, (span * span, 128), 1)
    source = idx_ref[0] * rows - rim + slot % ext
    inside = (source >= 0) & (source < nlat) & (slot < span * ext)
    for i in range(rows):
        total = jnp.zeros((k_pad, 128), f32)
        for line in range(i, i + span) if adjoint else (i + rim,):
            if adjoint:
                hit = (span - 1 - tap // span == slot // ext) & (slot % ext == line)
                hit = hit & (tap % span == i - line + span - 1)
            else:
                hit = (tap // span == slot // ext) & (slot % ext == i + tap % span)
            place = jnp.where(inside & hit, 1.0, 0.0).astype(bf16)
            total = total + dot(stencil_ref[line * k_pad : (line + 1) * k_pad, :], place)
        band[i * k_pad : (i + 1) * k_pad, :] = total.astype(bf16)

    depth = width * k_pad
    pair_row = lax.broadcasted_iota(jnp.int32, (taps * width, depth), 0)
    pair_lane = lax.broadcasted_iota(jnp.int32, (taps * width, depth), 1)
    place = jnp.where(
        pair_lane == (pair_row % width) * k_pad + pair_row // width, 1.0, 0.0
    ).astype(bf16)
    for g in range(groups):
        blend[g] = dot(mix_ref[g], place, TN).astype(bf16)


def conv_weights(where, stencil, mix, rim, nlat, adjoint):
    groups, _, width = mix.shape
    return pl.pallas_call(
        functools.partial(weights_kernel, rim, nlat, adjoint),
        out_shape=(
            jax.ShapeDtypeStruct((stencil.shape[0] - 32 * rim, 128), bf16),
            jax.ShapeDtypeStruct((groups, width, width * 16), bf16),
        ),
        in_specs=[pl.BlockSpec(memory_space=pltpu.SMEM)] + vmem(2),
        out_specs=tuple(vmem(2)),
        compiler_params=params(),
        cost_estimate=cost(4e8, 1e6),
        name="conv_weights",
    )(where, stencil, mix)


def conv_body(
    x_ref, low_ref, high_ref, left_ref, right_ref, band_ref, blend_ref, xs, hs, resp, emit
):
    rows, channels, cols = x_ref.shape
    groups, width, _ = blend_ref.shape
    ext = hs.shape[0] // channels
    rim = (ext - rows) // 2
    span = 2 * rim + 1
    edge = rim * channels // 128
    k_pad = 16
    xs[0 : rim * channels, :] = low_ref[0 : rim * channels].astype(f32)
    xs[rim * channels : (rim + rows) * channels, :] = (
        x_ref[...].astype(f32).reshape(rows * channels, cols)
    )
    xs[(rim + rows) * channels :, :] = high_ref[0 : rim * channels].astype(f32)

    row = lax.broadcasted_iota(jnp.int32, (16, cols), 0)
    lane = lax.broadcasted_iota(jnp.int32, (16, cols), 1)

    def spread(left, right, chunks, base):
        turned = jnp.transpose(jnp.concatenate([left.astype(f32), right.astype(f32)], axis=0))
        turned = turned.astype(bf16)
        for v, chunk in enumerate(chunks):
            ahead = (row - 2 * v == lane - (cols - 2)) & (lane >= cols - 2)
            behind = (row - 8 - 2 * v == lane) & (lane < 2)
            put = jnp.where(ahead | behind, 1.0, 0.0).astype(bf16)
            at = (base + chunk) * 128
            hs[at : at + 128, :] = dot(turned, put)

    lists = chunk_blocks(rows * channels // 128, edge)
    tail = rim * channels
    spread(low_ref[tail : tail + 8], low_ref[tail + 8 : tail + 16], range(edge), 0)
    spread(high_ref[tail : tail + 8], high_ref[tail + 8 : tail + 16], range(edge),
           edge + rows * channels // 128)
    for u, chunks in enumerate(lists):
        at = slice(8 * u, 8 * u + 8)
        spread(left_ref[at], right_ref[at], chunks, edge)

    stencil = band_ref[:, 0 : span * ext]

    def column(c):
        x = xs[pl.ds(c, ext, stride=channels), :]
        h = hs[pl.ds(c, ext, stride=channels), :]
        pieces = []
        for s in range(-rim, rim + 1):
            if s == 0:
                pieces.append(x)
                continue
            beyond = lane < s if s > 0 else lane >= cols + s
            pieces.append(pltpu.roll(jnp.where(beyond, h, x), (-s) % cols, 1))
        return jnp.concatenate([p.astype(bf16) for p in pieces], axis=0)

    for g in range(groups):

        def pair(number, carry):
            c = g * width + 2 * number
            both = jnp.concatenate([column(c), column(c + 1)], axis=1)
            r = dot(stencil, both).astype(bf16)
            at = pl.multiple_of(number * 2 * k_pad, k_pad)
            resp[:, pl.ds(at, k_pad), :] = r[:, 0:cols].reshape(rows, k_pad, cols)
            resp[:, pl.ds(at + k_pad, k_pad), :] = r[:, cols:].reshape(rows, k_pad, cols)
            return carry

        lax.fori_loop(0, width // 2, pair, 0, unroll=8)
        for i in range(0, rows, 2):
            operand = jnp.concatenate([resp[i], resp[i + 1]], axis=1)
            out = dot(blend_ref[g], operand)
            emit(g, i, out[:, 0:cols])
            emit(g, i + 1, out[:, cols:])


def forward_kernel(rim, nlat, *refs):
    where_ref, stencil_ref, mix_ref = refs[:3]
    act_ref, slope_ref, xs, hs, resp, band, blend = refs[8:]
    weights_kernel(rim, nlat, False, where_ref, stencil_ref, mix_ref, band, blend)
    width = blend.shape[1]
    chans = act_ref.shape[2]
    root = math.sqrt(2.0 / math.pi)

    def emit(g, i, v):
        square = v * v
        t = jnp.tanh(root * v * (1.0 + 0.044715 * square))
        half = 0.5 * (1.0 + t)
        act = v * half
        slope_ref[i, g * width : (g + 1) * width, :] = half + 0.5 * v * (1.0 - t * t) * (
            root + (root * 3.0 * 0.044715) * square
        )
        for j in range(width // chans):
            act_ref[g * (width // chans) + j, i] = act[j * chans : (j + 1) * chans, :].astype(bf16)

    conv_body(*refs[3:8], band, blend, xs, hs, resp, emit)


def adjoint_kernel(*refs):
    cot_ref, grad_ref = refs[7:9]
    width = refs[6].shape[1]

    def emit(g, i, v):
        at = slice(g * width, (g + 1) * width)
        grad_ref[i, at, :] = (cot_ref[i, at, :].astype(f32) + v).astype(bf16)

    conv_body(*refs[:7], *refs[9:12], emit)


def conv_scratch(rim, x, width):
    rows, channels, cols = x.shape
    flat = (rows + 2 * rim) * channels
    return [
        pltpu.VMEM((flat, cols), f32),
        pltpu.VMEM((flat, cols), f32),
        pltpu.VMEM((rows, width * 16, cols), bf16),
    ]


def conv_forward(where, stencil, mix, rim, nlat, x, halo, shape):
    groups, _, width = mix.shape
    return pl.pallas_call(
        functools.partial(forward_kernel, rim, nlat),
        out_shape=(jax.ShapeDtypeStruct(shape, bf16), jax.ShapeDtypeStruct(x.shape, f32)),
        in_specs=[pl.BlockSpec(memory_space=pltpu.SMEM)] + vmem(7),
        out_specs=tuple(vmem(2)),
        scratch_shapes=[
            *conv_scratch(rim, x, width),
            pltpu.VMEM((x.shape[0] * 16, 128), bf16),
            pltpu.VMEM((groups, width, width * 16), bf16),
        ],
        compiler_params=params(),
        cost_estimate=cost(1.2e10, 4e6),
        name="conv_forward",
    )(where, stencil, mix, x, *halo)


def conv_adjoint(weights, rim, x, halo, cot):
    return pl.pallas_call(
        adjoint_kernel,
        out_shape=jax.ShapeDtypeStruct(x.shape, bf16),
        in_specs=vmem(8),
        out_specs=vmem(1)[0],
        scratch_shapes=conv_scratch(rim, x, weights[1].shape[1]),
        compiler_params=params(),
        cost_estimate=cost(1.2e10, 4e6),
        name="conv_adjoint",
    )(x, *halo, *weights, cot)


def shifted(axis, step):
    count = lax.axis_size(axis)
    return [(a, (a + step) % count) for a in range(count)]


def lat_rims(x, left, right, rim):
    rows, channels, cols = x.shape
    low = jnp.concatenate([x[-rim:].reshape(rim * channels, cols), left[-8:], right[-8:]], axis=0)
    high = jnp.concatenate([x[:rim].reshape(rim * channels, cols), left[:8], right[:8]], axis=0)
    low = lax.ppermute(low, "lat", shifted("lat", 1))
    high = lax.ppermute(high, "lat", shifted("lat", -1))
    return low, high, left, right


def slope_kernel(edge, act_ref, slope_ref, out_ref, left_ref, right_ref):
    blocks, rows, chans, cols = act_ref.shape
    channels = blocks * chans

    def one(i, carry):
        parts = [act_ref[b, i].astype(f32) for b in range(blocks)]
        out_ref[i] = (slope_ref[i] * jnp.concatenate(parts, axis=0)).astype(bf16)
        return carry

    lax.fori_loop(0, rows, one, 0)
    first, last = edge_blocks(out_ref[...].reshape(rows * channels, cols), edge)
    left_ref[...] = first.astype(bf16)
    right_ref[...] = last.astype(bf16)


def slope_step(cot_act, slope, edge):
    rows, channels, cols = slope.shape
    blocks = len(chunk_blocks(rows * channels // 128, edge))
    shape = jax.ShapeDtypeStruct((8 * blocks, cols), bf16)
    return pl.pallas_call(
        functools.partial(slope_kernel, edge),
        out_shape=(jax.ShapeDtypeStruct(slope.shape, bf16), shape, shape),
        in_specs=vmem(2),
        out_specs=tuple(vmem(3)),
        compiler_params=params(),
        cost_estimate=cost(1e8, 3e6),
        name="slope_step",
    )(cot_act, slope)


def stencil_rows(weights):
    rows, span, _, k_count = weights.shape
    w = jnp.transpose(weights, (0, 3, 2, 1)).reshape(rows, k_count, span * span)
    w = jnp.pad(w, ((0, 0), (0, 16 - k_count), (0, 0)))
    return w.reshape(rows * 16, span * span).astype(bf16)


def local(input_field, basis_values, support_reach, mix_weight, filter_weight, cotangent):
    _, rows, channels, cols = input_field.shape
    rim = basis_values.shape[1] // 2
    degrees = filter_weight.shape[0]
    groups, k_count, width, _ = mix_weight.shape
    lat_count = lax.axis_size("lat")
    lon_count = lax.axis_size("lon")
    nlat = rows * lat_count
    nlon = cols * lon_count
    lat_index = lax.axis_index("lat")
    lon_index = lax.axis_index("lon")
    m_count = degrees // lat_count
    chans = channels // lon_count
    row_start = lat_index * rows
    field = input_field[0]
    cot = cotangent[0]

    edge = rim * channels // 128
    body = rows * chans

    sent = start_step(lon_index, cot, field, lon_count, edge)
    circ_c = lax.all_to_all(sent, "lon", 0, 0, tiled=True)

    blocks = 8 * len(chunk_blocks(rows * channels // 128, edge))
    strips = circ_c[:, body : body + blocks]
    left = lax.dynamic_index_in_dim(strips, (lon_index + lon_count - 1) % lon_count, 0, False)
    right = lax.dynamic_index_in_dim(strips, (lon_index + 1) % lon_count, 0, False)
    offsets = jnp.abs(jnp.arange(2 * rim + 1, dtype=jnp.int32) - rim)
    pad = ((rim, rim), (0, 0), (0, 0), (0, 0))
    basis_ext = lax.dynamic_slice_in_dim(jnp.pad(basis_values, pad), row_start, rows + 2 * rim, 0)
    reach_ext = lax.dynamic_slice_in_dim(
        jnp.pad(support_reach, pad[:2]), row_start, rows + 2 * rim, 0
    )
    inside = offsets[None, None, :] <= reach_ext[:, :, None]
    weights_ext = jnp.where(inside[..., None], basis_ext, 0.0)
    stencil = stencil_rows(weights_ext)
    mix = mix_weight.reshape(groups, k_count * width, width)
    mix_adj = jnp.transpose(mix_weight, (0, 1, 3, 2)).reshape(groups, k_count * width, width)
    where = lat_index[None]
    tab = lon_table(degrees, nlon, lat_count)
    legendre = legendre_inputs(degrees, lat_count, rows)
    theta = math.pi * (np.arange(nlat) + 0.5) / nlat
    quad = 2.0 * math.pi * math.pi / nlat * np.sin(theta) / nlon
    quad_rows = np.repeat(quad.reshape(lat_count, rows), chans, axis=1).astype(np.float32)
    post = np.broadcast_to(quad.reshape(lat_count, rows).T.reshape(nlat, 1), (nlat, 128))
    post = jnp.asarray(post.astype(np.float32))
    here = lat_index[None]
    shape = (lon_count, rows, chans, cols)

    table = legendre_table(here, legendre, m_count, degrees, nlat)
    circ_c, table = lax.optimization_barrier((circ_c, table))
    send_1 = analysis(circ_c, body, tab, lat_count)
    halo = lat_rims(field, left, right, rim)
    send_1, halo = lax.optimization_barrier((send_1, halo))
    recv_1 = lax.all_to_all(send_1, "lat", 0, 0, tiled=True)
    act, slope = conv_forward(where, stencil, mix, rim, nlat, field, halo, shape)
    act, table, filter_weight, later = lax.optimization_barrier(
        (act, table, filter_weight, lat_index)
    )
    quad_lanes = lax.dynamic_slice_in_dim(jnp.asarray(quad_rows), later, 1, 0)
    flip = flipped_table(table)
    recv_1, act, table, flip = lax.optimization_barrier((recv_1, act, table, flip))
    circ_f = lax.all_to_all(act, "lon", 0, 0, tiled=True)
    filtered_c = filter_step(here, lon_index[None], recv_1, filter_weight, post, table, flip, chans, True)
    send_2 = analysis(circ_f, body, tab, lat_count, quad_lanes, filtered_c)
    recv_2 = lax.all_to_all(send_2, "lat", 0, 0, tiled=True)
    stencil, send_2 = lax.optimization_barrier((stencil, send_2))
    weights_adj = conv_weights(where, stencil, mix_adj, rim, nlat, True)
    recv_2, weights_adj = lax.optimization_barrier((recv_2, weights_adj))
    cot_act = lax.all_to_all(synthesis(recv_2, tab, 1, shape), "lon", 0, 0, tiled=True)
    filtered_f = filter_step(here, lon_index[None], recv_2, filter_weight, post, table, flip, chans, False)
    recv_3 = lax.all_to_all(filtered_f, "lat", 0, 0, tiled=True)
    branch = lax.all_to_all(synthesis(recv_3, tab, 0, shape), "lon", 0, 0, tiled=True)

    cot_conv, first_c, last_c = slope_step(cot_act, slope, edge)
    left_c = lax.ppermute(last_c, "lon", shifted("lon", 1))
    right_c = lax.ppermute(first_c, "lon", shifted("lon", -1))
    halo_c = lat_rims(cot_conv, left_c, right_c, rim)
    grad_field = conv_adjoint(weights_adj, rim, cot_conv, halo_c, cot)
    branch = jnp.transpose(branch, (1, 0, 2, 3)).reshape(rows, channels, cols)
    block_out = (field.astype(f32) + branch.astype(f32)).astype(bf16)
    return block_out[None], grad_field[None]


def solution(mesh):
    placed = (P(None, "lat", None, "lon"), P(), P(), P(), P(), P(None, "lat", None, "lon"))
    return jax.shard_map(
        local,
        mesh=mesh,
        in_specs=placed,
        out_specs=(P(None, "lat", None, "lon"), P(None, "lat", None, "lon")),
        check_vma=False,
    )
```
